256 devices in a mesh: seq: 32 (over x, z), head: 8 (over y, core).
Axes of the slice: x: 4, y: 4, z: 8, core: 2. Of those that a mesh axis runs over, the one named last changes fastest.
Arguments:
- projected: bfloat16 [3, 16384, 4096], P(None, 'seq', 'head'), may hold values from -6 to 6
- conv_weight: float32 [3, 4, 4096], P(None, None, 'head'), may hold values from -3 to 3
- out_weight: bfloat16 [4096, 4096], P('head'), may hold values from -0.09375 to 0.09375
- out_grad: bfloat16 [16384, 4096], P('seq', 'head'), may hold values from -6 to 6
- doc_lengths: int32 [8], replicated, may hold values from 1 to 4096, 16384 in all
Outputs:
- mixed: bfloat16 [16384, 4096], P('seq', 'head')
- grad_projected: bfloat16 [3, 16384, 4096], P(None, 'seq', 'head')
- grad_conv: float32 [3, 4, 4096], P(None, None, 'head')
- grad_out_weight: float32 [4096, 4096], P('head', 'seq')
The draws below stay inside these ranges and needn't reach their ends.
Inputs may be any that keep to these rules, and one draw needn't show every extreme that they name: `doc_lengths`: the lengths sum to 16384 and the longest is exactly 4096.
All inputs are finite; a program needn't handle non-finite values.
Results may differ from the reference program's by a relative error of at most 0.017.
Values may be sent and summed in bfloat16 or wider, within the bound.
A program may use at most 128 MiB of HBM per device.

```python
import math
import jax
import jax.numpy as jnp
import numpy as np
from jax import lax

D = 4096
HEADS = 32
DH = 128
KW = 4
HIDDEN_SIZE = 4096
TOKENS = 16384
DOCS = 8
N_HEAD = 8


def strengthened(drawn, key, source, target, parts, factor):
    owner, partner = [(jnp.arange(drawn.shape[dim]) // (drawn.shape[dim] // parts)).reshape([-1 if axis == dim else 1 for axis in range(drawn.ndim)]) for dim in (source, target)]
    chosen = jax.random.permutation(key, parts)[partner]
    strong = (owner == chosen) | (owner == (partner + parts // 2) % parts)
    return jnp.where(strong, factor * drawn, drawn)


def block_scale(stream_key, dims, cuts, least, top_value):
    factor_of = 1.0
    for position, shards_of in cuts:
        heights = jax.random.uniform(jax.random.fold_in(jax.random.fold_in(stream_key, 6), position), (shards_of,), jnp.float32, least / len(cuts), top_value / len(cuts))
        factor_of = factor_of * jnp.repeat(jnp.exp(heights), dims[position] // shards_of).reshape((-1,) + (1,) * (len(dims) - 1 - position))
    return factor_of


def profile(number_of, total, reach, lean):
    loads = [(1 << 20) // math.isqrt(rank ** lean) + 1 for rank in range(2, number_of + 1)]
    surplus, holding = total - reach - (number_of - 1), [1] * (number_of - 1)
    while surplus > 0:
        candidates = [i for i in range(number_of - 1) if holding[i] < reach]
        whole, left = sum([loads[i] for i in candidates]), surplus
        for i in candidates:
            addition = min(reach - holding[i], max(1, left * loads[i] // whole), surplus)
            holding[i] = holding[i] + addition
            surplus = surplus - addition
    return np.array([reach] + holding)


def ragged(rng, amount, total, most, skew):
    if amount == 2:
        one = jax.random.randint(rng, (), max(1, total - most), min(most, total - 1) + 1)
        return jnp.stack([one, total - one])
    lengths = jnp.asarray(profile(amount, total, most, skew), jnp.int32)
    pairs = (amount - 1) // 2
    source_of, taker = lengths[1:1 + 2 * pairs:2], lengths[2:2 + 2 * pairs:2]
    margin = jnp.minimum(source_of - 1, most - taker)
    moved = jax.random.randint(jax.random.fold_in(rng, 1), (pairs,), 0, 1 << 20) % (margin + 1)
    lengths = lengths.at[1:1 + 2 * pairs:2].set(source_of - moved).at[2:2 + 2 * pairs:2].set(taker + moved)
    return lengths[jax.random.permutation(jax.random.fold_in(rng, 2), amount)]


def normal_values(stream_key, shape, deviation, reach, cuts=(), kind=jnp.bfloat16):
    drawn = jax.random.normal(stream_key, shape, jnp.float32) * deviation
    if len(cuts) > 0:
        drawn = block_scale(stream_key, shape, cuts, -0.22, 0.18) * drawn
    return jnp.clip(drawn, min=-reach, max=reach).astype(kind)


def gaussian_with(stream_key, dims, spread, limit, cuts, heavy, kind=jnp.bfloat16):
    values = spread * jax.random.normal(stream_key, dims, jnp.float32)
    if cuts:
        values = values * block_scale(stream_key, dims, cuts, -0.22, 0.18)
    return jnp.clip(strengthened(values, jax.random.fold_in(stream_key, 3), *heavy), -limit, limit).astype(kind)


def setup_inputs(seed: int = 0) -> dict:
    streams_of = jax.random.split(jax.random.key(seed), 6)
    return {
        "projected": normal_values(streams_of[0], (3, TOKENS, HIDDEN_SIZE), 1.0, 6.0, ((1, 32), (2, 8))),
        "conv_weight": normal_values(streams_of[1], (3, KW, HIDDEN_SIZE), KW ** -0.5, 3.0, ((2, 8),), jnp.float32),
        "out_weight": normal_values(streams_of[2], (HIDDEN_SIZE, D), HIDDEN_SIZE ** -0.5, 0.09375, ((0, 8),)),
        "out_grad": gaussian_with(streams_of[3], (TOKENS, D), 1.0, 6.0, ((0, 32), (1, 8)), (0, 1, 32, 2.75)),
        "doc_lengths": ragged(streams_of[4], DOCS, TOKENS, TOKENS // 4, 2).astype(jnp.int32),
    }


def doc_index(doc_lengths, positions):
    doc_starts = jnp.cumsum(doc_lengths) - doc_lengths
    counted = lax.optimization_barrier(jnp.sum((doc_starts[None, :] <= positions[:, None]).astype(jnp.int32), axis=1))
    return (counted - 1).astype(jnp.int32)

def lagged(field, shift_by, fill):
    padding = jnp.full((shift_by,) + field.shape[1:], fill, field.dtype)
    return jnp.concatenate([padding, field[:field.shape[0] - shift_by]], axis=0)

def leading(field, shift_by, fill):
    padding = jnp.full((shift_by,) + field.shape[1:], fill, field.dtype)
    return jnp.concatenate([field[shift_by:], padding], axis=0)

def feature_map(field):
    return jax.nn.elu(field) + 1.0

def attend(queries, keys, values, doc_ids):
    block = math.gcd(TOKENS, 512)
    count = TOKENS // block
    places = jnp.arange(block)
    high = lax.Precision.HIGHEST
    queries = feature_map(queries)
    keys = feature_map(keys)

    def one_block(carry, pieces):
        state, prior = carry
        q_block, k_block, v_block, ids = pieces
        scores = jnp.einsum('thd,shd->hts', q_block, k_block, precision=high)
        allowed = (places[None, :] <= places[:, None]) & (ids[:, None] == ids[None, :])
        weights = jnp.where(allowed[None], scores, 0.0)
        result = jnp.einsum('hts,shd->thd', weights, v_block, precision=high)
        head_mask = (ids == prior).astype(jnp.float32)
        result = result + head_mask[:, None, None] * jnp.einsum('thd,hde->the', q_block, state, precision=high)
        tail_mask = (ids == ids[-1]).astype(jnp.float32)
        local = jnp.einsum('thd,the->hde', k_block * tail_mask[:, None, None], v_block, precision=high)
        kept = (ids[-1] == prior).astype(jnp.float32)
        return ((local + kept * state, ids[-1]), result)
    pieces = (queries.reshape(count, block, HEADS, DH), keys.reshape(count, block, HEADS, DH), values.reshape(count, block, HEADS, DH), doc_ids.reshape(count, block))
    start = (jnp.zeros((HEADS, DH, DH), jnp.float32), jnp.int32(-1))
    final_carry, outs = lax.scan(jax.checkpoint(one_block), start, pieces)
    outputs = outs.reshape(TOKENS, HEADS, DH)
    scale = lax.rsqrt(lax.optimization_barrier(jnp.mean(outputs * outputs, axis=-1, keepdims=True)) + 1e-06)
    return (outputs * scale).reshape(TOKENS, HIDDEN_SIZE)

def reference(projected, conv_weight, out_weight, out_grad, doc_lengths):
    doc_ids = doc_index(doc_lengths, jnp.arange(TOKENS, dtype=jnp.int32))
    acts = []
    for stream in range(3):
        raw = projected[stream].astype(jnp.float32)
        total = jnp.zeros((TOKENS, HIDDEN_SIZE), jnp.float32)
        for tap in range(KW):
            kept = (lagged(doc_ids, tap, -1) == doc_ids).astype(jnp.float32)
            total = total + conv_weight[stream, tap][None, :] * lagged(raw, tap, 0.0) * kept[:, None]
        acts.append(total.astype(jnp.bfloat16))
    attend_docs = lambda queries, keys, values: attend(queries, keys, values, doc_ids)
    unit, pullback = jax.vjp(attend_docs, acts[0].astype(jnp.float32), acts[1].astype(jnp.float32), acts[2].astype(jnp.float32))
    normed = unit.astype(jnp.bfloat16)
    group = HIDDEN_SIZE // N_HEAD
    summed = jnp.zeros((TOKENS, D), jnp.float32)
    for index in range(N_HEAD):
        partial_sum = jnp.dot(normed[:, index * group:(index + 1) * group], out_weight[index * group:(index + 1) * group], preferred_element_type=jnp.float32).astype(jnp.bfloat16)
        partial_sum = lax.optimization_barrier(partial_sum)
        summed = summed + partial_sum.astype(jnp.float32)
    mixed = summed.astype(jnp.bfloat16)
    grad_out_weight = jnp.dot(normed.T, out_grad, preferred_element_type=jnp.float32)
    grad_unit = jnp.dot(out_grad, out_weight.T, preferred_element_type=jnp.float32)
    grad_acts = pullback(grad_unit)
    grad_list = []
    conv_list = []
    for stream in range(3):
        raw = projected[stream].astype(jnp.float32)
        grad = grad_acts[stream]
        d_raw = jnp.zeros((TOKENS, HIDDEN_SIZE), jnp.float32)
        taps = []
        for tap in range(KW):
            kept = (lagged(doc_ids, tap, -1) == doc_ids).astype(jnp.float32)
            masked = grad * kept[:, None]
            d_raw = d_raw + conv_weight[stream, tap][None, :] * leading(masked, tap, 0.0)
            taps.append(lax.optimization_barrier(jnp.sum(masked * lagged(raw, tap, 0.0), axis=0)))
        grad_list.append(d_raw.astype(jnp.bfloat16))
        conv_list.append(jnp.stack(taps, axis=0))
    return (mixed, jnp.stack(grad_list, axis=0), jnp.stack(conv_list, axis=0), grad_out_weight)
```

```python
import jax
import jax.numpy as jnp
from jax import lax
from jax.sharding import PartitionSpec as P

DH = 128
KW = 4


def from_behind(array, axis, by):
    peers = lax.axis_size(axis)
    pairs = [(i, i + by) for i in range(peers) if 0 <= i + by < peers]
    return lax.ppermute(array, axis, pairs)


def segment_of(doc_starts, positions):
    counted = jnp.sum((doc_starts[None, :] <= positions[:, None]).astype(jnp.int32), axis=1)
    return counted - 1


def window_carry(local, doc_end, step):
    total = from_behind(local, "seq", step)
    reach = 1
    while reach < 8:
        total = total + doc_end(reach) * from_behind(total, "seq", step * reach)
        reach *= 2
    return total


def feature_map(field):
    return jax.nn.elu(field) + 1.0


def feature_slope(field):
    return jnp.where(field > 0, 1.0, jnp.exp(jnp.minimum(field, 0.0)))


def body(projected, conv_weight, out_weight, out_grad, doc_lengths):
    tok_rows = projected.shape[1]
    channels = projected.shape[2]
    head_count = channels // DH
    high = lax.Precision.DEFAULT
    offset = lax.axis_index("seq") * tok_rows
    doc_starts = jnp.cumsum(doc_lengths) - doc_lengths
    positions = offset + jnp.arange(-(KW - 1), tok_rows + KW - 1, dtype=jnp.int32)
    doc_all = segment_of(doc_starts, positions)
    block_ends = offset + tok_rows * jnp.arange(-8, 9, dtype=jnp.int32) - 1
    doc_at = segment_of(doc_starts, block_ends)
    behind = lambda reach: (doc_at[8] == doc_at[8 - reach]).astype(jnp.float32)
    ahead_of = lambda reach: (doc_at[9] == doc_at[9 + reach]).astype(jnp.float32)
    doc_here = doc_all[KW - 1 : KW - 1 + tok_rows]
    doc_before = doc_all[KW - 2]
    doc_last = doc_all[KW - 2 + tok_rows]
    rim = from_behind(projected[:, tok_rows - (KW - 1) :, :], "seq", 1)
    extended = jnp.concatenate([rim, projected], axis=1)
    conv_sum = jnp.zeros((3, tok_rows, channels), jnp.float32)
    masks = []
    for tap in range(KW):
        kept = (doc_all[KW - 1 - tap : KW - 1 - tap + tok_rows] == doc_here).astype(jnp.float32)
        masks.append(kept)
        conv_sum = (
            conv_sum
            + conv_weight[:, tap, None, :]
            * extended[:, KW - 1 - tap : KW - 1 - tap + tok_rows, :]
            * kept[None, :, None]
        )
    acts = conv_sum.astype(jnp.bfloat16)
    query_raw = acts[0].reshape(tok_rows, head_count, DH).astype(jnp.float32)
    key_raw = acts[1].reshape(tok_rows, head_count, DH).astype(jnp.float32)
    value_float = acts[2].reshape(tok_rows, head_count, DH).astype(jnp.float32)
    query_float = feature_map(query_raw)
    key_float = feature_map(key_raw)
    places = jnp.arange(tok_rows)
    allowed = (places[None, :] <= places[:, None]) & (doc_here[:, None] == doc_here[None, :])
    scores = jnp.einsum("thd,shd->hts", query_float, key_float, precision=high)
    weights = jnp.where(allowed[None], scores, 0.0)
    local_out = jnp.einsum("hts,shd->thd", weights, value_float, precision=high)
    head_mask = (doc_here == doc_before).astype(jnp.float32)[:, None, None]
    tail_keep = doc_here == doc_last
    tail_mask = tail_keep.astype(jnp.float32)[:, None, None]
    tail_state = jnp.einsum("thd,the->hde", key_float * tail_mask, value_float, precision=high)
    state_in = window_carry(tail_state, behind, 1)
    outputs = local_out + head_mask * jnp.einsum(
        "thd,hde->the", query_float, state_in, precision=high
    )
    scale = lax.rsqrt(jnp.mean(outputs * outputs, axis=-1, keepdims=True) + 1e-06)
    unit = outputs * scale
    normed = unit.reshape(tok_rows, channels).astype(jnp.bfloat16)
    columns = out_weight
    summed = lax.psum_scatter(
        lax.dot_general(
            columns, normed, (((0,), (1,)), ((), ())), preferred_element_type=jnp.float32
        ).astype(jnp.bfloat16),
        "head",
        scatter_dimension=0,
        tiled=True,
    ).astype(jnp.float32)
    mixed = summed.T.astype(jnp.bfloat16)
    full_grad = lax.all_gather(out_grad, "head", axis=1, tiled=True)
    columns = full_grad
    grad_out_weight = lax.psum_scatter(
        lax.dot_general(
            columns, normed, (((0,), (0,)), ((), ())), preferred_element_type=jnp.float32
        ).astype(jnp.bfloat16),
        "seq",
        scatter_dimension=0,
        tiled=True,
    ).astype(jnp.float32).T
    grad_unit = lax.dot_general(
        full_grad, out_weight, (((1,), (1,)), ((), ())), preferred_element_type=jnp.float32
    )
    grad_unit = grad_unit.reshape(tok_rows, head_count, DH)
    grad_outputs = scale * (grad_unit - unit * jnp.mean(grad_unit * unit, axis=-1, keepdims=True))
    grad_weights = jnp.where(
        allowed[None], jnp.einsum("thd,shd->hts", grad_outputs, value_float, precision=high), 0.0
    )
    grad_back = jnp.einsum("thd,the->hde", query_float * head_mask, grad_outputs, precision=high)
    state_out = window_carry(grad_back, ahead_of, -1)
    grad_query = jnp.einsum("hts,shd->thd", grad_weights, key_float, precision=high)
    grad_query = grad_query + head_mask * jnp.einsum(
        "the,hde->thd", grad_outputs, state_in, precision=high
    )
    grad_query = grad_query * feature_slope(query_raw)
    grad_key = jnp.einsum("hts,thd->shd", grad_weights, query_float, precision=high)
    grad_key = grad_key + tail_mask * jnp.einsum(
        "hde,she->shd", state_out, value_float, precision=high
    )
    grad_key = grad_key * feature_slope(key_raw)
    grad_value = jnp.einsum("hts,thd->shd", weights, grad_outputs, precision=high)
    grad_value = grad_value + tail_mask * jnp.einsum(
        "shd,hde->she", key_float, state_out, precision=high
    )
    grad_acts = jnp.stack([grad_query, grad_key, grad_value], axis=0).reshape(3, tok_rows, channels)
    ahead = from_behind(grad_acts[:, : KW - 1, :], "seq", -1)
    grad_ext = jnp.concatenate([grad_acts, ahead], axis=1)
    grad_raw = jnp.zeros((3, tok_rows, channels), jnp.float32)
    tap_sums = []
    for tap in range(KW):
        kept_next = (doc_all[KW - 1 + tap : KW - 1 + tap + tok_rows] == doc_here).astype(
            jnp.float32
        )
        grad_raw = (
            grad_raw
            + conv_weight[:, tap, None, :]
            * grad_ext[:, tap : tap + tok_rows, :]
            * kept_next[None, :, None]
        )
        lagged_raw = extended[:, KW - 1 - tap : KW - 1 - tap + tok_rows, :]
        tap_sums.append(jnp.sum(grad_acts * lagged_raw * masks[tap][None, :, None], axis=1))
    grad_conv = lax.psum(jnp.stack(tap_sums, axis=1), "seq")
    return (mixed, grad_raw.astype(jnp.bfloat16), grad_conv, grad_out_weight)


def solution(mesh):
    return jax.shard_map(
        body,
        mesh=mesh,
        in_specs=(
            P(None, "seq", "head"),
            P(None, None, "head"),
            P("head", None),
            P("seq", "head"),
            P(),
        ),
        out_specs=(
            P("seq", "head"),
            P(None, "seq", "head"),
            P(None, None, "head"),
            P("head", "seq"),
        ),
        check_vma=False,
    )
```

```python
import jax
import jax.numpy as jnp
from jax import lax
from jax.experimental import pallas as pl
from jax.experimental.pallas import tpu as pltpu
from jax.sharding import PartitionSpec as P

DH = 128
KW = 4
HEADS = 4
ROWS = 512
WIDTH = 512
DOCS = 8
TOKENS = 16384
NX, NZ, NY = 4, 8, 4
EDGE = 16
BF = jnp.bfloat16
F32 = jnp.float32
MESH = pl.DeviceIdType.MESH
COPIES = 112

LANES = [pl.ds(h * DH, DH) for h in range(HEADS)]


def wrap(value, size):
    return lax.rem(value + size, size)


def lanes_of(head):
    return pl.ds(pl.multiple_of(head * DH, DH), DH)


def dot(a, b, left=1, right=0):
    return lax.dot_general(a, b, (((left,), (right,)), ((), ())), preferred_element_type=F32)


class Links:
    def __init__(self, send_sems, recv_sems):
        self.send_sems, self.recv_sems = send_sems, recv_sems
        self.used, self.pending = 0, []

    def start(self, source, target, device):
        copy = pltpu.make_async_remote_copy(
            src_ref=source,
            dst_ref=target,
            send_sem=self.send_sems.at[self.used],
            recv_sem=self.recv_sems.at[self.used],
            device_id=device,
            device_id_type=MESH,
        )
        self.used += 1
        copy.start()
        self.pending.append(copy)
        return copy

    def drain(self):
        for copy in self.pending:
            copy.wait_send()


def add_into(target, source):
    for tile in range(target.shape[0]):
        target[tile] = (target[tile].astype(F32) + source[tile].astype(F32)).astype(BF)


class Ring:
    def __init__(self, links, n, me, device_of, own, halves, blocks):
        self.links, self.n, self.me = links, n, me
        self.device_of, self.own = device_of, own
        self.halves, self.blocks = halves, blocks
        self.arrivals = {}

    def part(self, way, ref, near):
        half = ref.shape[0] // 2
        first = (way == 0) == near
        return ref.at[pl.ds(0 if first else half, half)]

    def begin(self):
        far = self.n // 2
        for way, sign in ((0, 1), (1, -1)):
            there = self.device_of(wrap(self.me + sign, self.n))
            block = self.own(wrap(self.me + far, self.n))
            self.arrivals[way, 1] = [
                self.links.start(self.part(way, block, True), self.halves.at[way], there)
            ]
        for way, sign in ((0, 1), (1, -1)):
            there = self.device_of(wrap(self.me + sign, self.n))
            block = self.own(wrap(self.me + sign * (far - 1), self.n))
            self.arrivals[way, 2] = [
                self.links.start(
                    self.part(way, block, False),
                    self.part(way, self.blocks.at[way, 0], False),
                    there,
                )
            ]

    def relay(self, step):
        far = self.n // 2
        for way, sign in ((0, 1), (1, -1)):
            there = self.device_of(wrap(self.me + sign, self.n))
            block = self.own(wrap(self.me + sign * (far - step + 1), self.n))
            for copy in self.arrivals[way, step - 1]:
                copy.wait_recv()
            if step == 2:
                mine = self.part(way, block, True)
                add_into(mine, self.halves.at[way])
                landing = self.part(way, self.blocks.at[way, 0], True)
                self.arrivals[way, 2].append(self.links.start(mine, landing, there))
            else:
                add_into(block, self.blocks.at[way, step - 3])
                landing = self.blocks.at[way, step - 2]
                self.arrivals[way, step] = [self.links.start(block, landing, there)]

    def finish(self):
        last = self.n // 2
        for way in (0, 1):
            for copy in self.arrivals[way, last]:
                copy.wait_recv()
        return self.own(self.me), self.blocks.at[0, last - 2], self.blocks.at[1, last - 2]


def kernel(
    docs, proj_hbm, taps, weight_hbm, grad_hbm,
    mixed_out, gproj_out, gtaps_out, gweight_out,
    proj, weight, og, rim, grim,
    mask_back, mask_next, mask_head, mask_tail, allowed,
    qf, kf, val, probs, unit, scale, gunit, normed, normed_t, go, gprobs, gacts,
    fwd_send, fwd_in, fwd_row, fwd_rowin, fwd_out, state,
    bwd_send, bwd_in, bwd_row, bwd_rowin, bwd_out, gstate,
    sib_send, sib_recv, mix, mix_half, mix_block,
    gx, gx_half, gx_block, gx2, gx2_half, gx2_block,
    gz, gz_half, gz_block, gz2, gz2_half, gz2_block,
    tap_part, tap_in, tap_row, tap_rowin,
    local_sems, send_sems, recv_sems,
):
    seq, head = lax.axis_index("seq"), lax.axis_index("head")
    x, z = seq // NZ, lax.rem(seq, NZ)
    y, core = head // 2, lax.rem(head, 2)
    at_x = lambda to: (to * NZ + z, head)
    at_z = lambda to: (x * NZ + to, head)
    at_y = lambda to: (seq, to * 2 + core)
    sibling = (seq, y * 2 + (1 - core))
    token_next = (wrap(seq + 1, NX * NZ), head)
    token_prev = (wrap(seq - 1, NX * NZ), head)
    links = Links(send_sems, recv_sems)

    load_proj = pltpu.make_async_copy(proj_hbm, proj, local_sems.at[0])
    load_grad = pltpu.make_async_copy(grad_hbm, og.at[head], local_sems.at[1])
    load_weight = pltpu.make_async_copy(weight_hbm, weight, local_sems.at[2])
    load_grad.start()
    load_proj.start()
    load_weight.start()

    partners = [sibling, at_y(wrap(y + 1, NY)), at_y(wrap(y - 1, NY)), token_next, token_prev]
    partners += [at_x(wrap(x + k, NX)) for k in range(1, NX)]
    partners += [at_z(wrap(z + k, NZ)) for k in range(1, NZ)]
    barrier = pltpu.get_barrier_semaphore()
    for partner in partners:
        pl.semaphore_signal(barrier, inc=1, device_id=partner, device_id_type=MESH)

    starts = []
    total = jnp.int32(0)
    for i in range(DOCS):
        starts.append(total)
        total = total + docs[i]
    offset = seq * ROWS

    def doc_at(position):
        count = jnp.int32(0)
        for start in starts:
            count = count + jnp.where(start <= position, 1, 0)
        return count

    ends = [doc_at((x * NZ + k) * ROWS - 1) for k in range(NZ + 1)]
    same = lambda a, b: jnp.where(ends[a] == ends[b], jnp.float32(1), jnp.float32(0))

    position = offset + lax.broadcasted_iota(jnp.int32, (ROWS, DH), 0)
    doc_start = jnp.zeros((ROWS, DH), jnp.int32)
    doc_end = jnp.full((ROWS, DH), TOKENS, jnp.int32)
    for i in range(1, DOCS):
        doc_start = jnp.where(starts[i] <= position, starts[i], doc_start)
    for i in range(DOCS - 1, 0, -1):
        doc_end = jnp.where(starts[i] > position, starts[i], doc_end)
    one, zero = jnp.float32(1), jnp.float32(0)
    for j in range(1, KW):
        mask_back[j - 1] = jnp.where(position - j >= doc_start, one, zero)
        mask_next[j - 1] = jnp.where(position + j < doc_end, one, zero)
    mask_head[...] = jnp.where(doc_start < offset, one, zero)
    mask_tail[...] = jnp.where(doc_end > offset + ROWS - 1, one, zero)
    for tile in range(ROWS // DH):
        column = offset + tile * DH + lax.broadcasted_iota(jnp.int32, (ROWS, DH), 1)
        allowed[:, tile * DH : (tile + 1) * DH] = jnp.where(
            (column <= position) & (column >= doc_start), one, zero
        )

    load_grad.wait()
    pl.semaphore_wait(barrier, len(partners))

    half = ROWS // 2
    up, down, across = wrap(y + 1, NY), wrap(y - 1, NY), wrap(y + 2, NY)
    block_of = lambda to: to * 2 + core
    top = lambda to: og.at[block_of(to), pl.ds(0, half)]
    bottom = lambda to: og.at[block_of(to), pl.ds(half, half)]
    whole = lambda to: og.at[block_of(to)]
    up_top = links.start(top(y), top(y), at_y(up))
    down_bottom = links.start(bottom(y), bottom(y), at_y(down))
    up_bottom = links.start(bottom(y), bottom(y), at_y(up))
    down_top = links.start(top(y), top(y), at_y(down))
    load_proj.wait()
    rim_copy = links.start(proj.at[:, pl.ds(ROWS - EDGE, EDGE)], rim, token_next)
    sib_own = links.start(whole(y), whole(y), sibling)

    def activate(stream, acc, rows, lanes):
        act = acc.astype(BF)
        if stream == 2:
            val[rows, lanes] = act
        else:
            wide = act.astype(F32)
            feature = jnp.where(wide > 0, wide + 1.0, jnp.exp(jnp.minimum(wide, 0.0)))
            (qf, kf)[stream][rows, lanes] = feature.astype(BF)

    def convolve(number, _):
        lanes = lanes_of(number)
        for stream in range(3):
            raw = proj[stream, :, lanes].astype(F32)
            acc = taps[stream, 0:1, lanes] * raw
            for j in range(1, KW):
                acc = acc + taps[stream, j : j + 1, lanes] * (
                    pltpu.roll(raw, j, 0) * mask_back[j - 1]
                )
            activate(stream, acc, slice(None), lanes)
        return 0

    lax.fori_loop(0, HEADS, convolve, 0)
    rim_copy.wait_recv()

    def convolve_rim(number, _):
        lanes = lanes_of(number)
        for stream in range(3):
            raw = proj[stream, 0:EDGE, lanes].astype(F32)
            both = jnp.concatenate([rim[stream, :, lanes].astype(F32), raw], axis=0)
            acc = taps[stream, 0:1, lanes] * raw
            for j in range(1, KW):
                acc = acc + taps[stream, j : j + 1, lanes] * (
                    pltpu.roll(both, j, 0)[EDGE:] * mask_back[j - 1, 0:EDGE]
                )
            activate(stream, acc, slice(0, EDGE), lanes)
        return 0

    lax.fori_loop(0, HEADS, convolve_rim, 0)

    def tail_state(number, _):
        lanes = lanes_of(number)
        keys = (kf[:, lanes].astype(F32) * mask_tail[...]).astype(BF)
        local = dot(keys, val[:, lanes], 0, 0)
        fwd_send[pl.ds(2 * number, 2)] = local.astype(BF).reshape(2, DH // 2, DH)
        return 0

    def to_owners(send, landing):
        return [
            links.start(send.at[wrap(z + k, NZ)], landing.at[z], at_z(wrap(z + k, NZ)))
            for k in range(1, NZ)
        ]

    lax.fori_loop(0, HEADS, tail_state, 0)
    fwd_copies = to_owners(fwd_send, fwd_in)
    fwd_in[z] = fwd_send[z]

    up_top.wait_recv()
    pass_top = links.start(top(down), top(down), at_y(up))
    down_bottom.wait_recv()
    pass_bottom = links.start(bottom(up), bottom(up), at_y(down))

    def local_attention(number, _):
        lanes = lanes_of(number)
        for r in range(ROWS // DH):
            rows, width = slice(r * DH, (r + 1) * DH), (r + 1) * DH
            scores = dot(qf[rows, lanes], kf[0:width, lanes], 1, 1)
            kept = (scores * allowed[rows, 0:width]).astype(BF)
            probs[number, rows, 0:width] = kept
            unit[rows, lanes] = dot(kept, val[0:width, lanes])
        return 0

    lax.fori_loop(0, HEADS, local_attention, 0)

    for copy in fwd_copies:
        copy.wait_recv()
    run = jnp.zeros((DH // 2, DH), F32)
    prefix = []
    for k in range(NZ):
        prefix.append(run)
        run = fwd_in[k].astype(F32) + same(k, k + 1) * run
    fwd_row[...] = run.astype(BF)
    row_copy = links.start(fwd_row, fwd_rowin, at_x(wrap(x + 1, NX)))

    load_weight.wait()

    def add_gunit(block, first=False):
        columns = pl.ds(pl.multiple_of(block * WIDTH, WIDTH), WIDTH)

        def tile(r, _):
            rows = pl.ds(pl.multiple_of(r * 256, 256), 256)
            part = dot(og[block, rows, :], weight[:, columns], 1, 1)
            gunit[rows, :] = part if first else gunit[rows, :] + part
            return 0

        lax.fori_loop(0, ROWS // 256, tile, 0)

    add_gunit(block_of(y), True)
    row_copy.wait_recv()
    carried = fwd_rowin[...].astype(F32)
    for k in range(NZ):
        fwd_out[k] = (prefix[k] + same(k, 0) * carried).astype(BF)
    out_copies = to_owners(fwd_out, state)
    state[z] = fwd_out[z]

    other = lambda to: to * 2 + (1 - core)
    sib_own.wait_recv()
    add_gunit(other(y))
    up_bottom.wait_recv()
    sib_down = links.start(whole(down), whole(down), sibling)
    down_top.wait_recv()
    sib_up = links.start(whole(up), whole(up), sibling)
    add_gunit(block_of(down))
    add_gunit(block_of(up))

    for copy in out_copies:
        copy.wait_recv()

    def finish_attention(number, _):
        lanes = lanes_of(number)
        carried_in = state[pl.ds(2 * number, 2)].reshape(DH, DH)
        attn = unit[:, lanes] + mask_head[...] * dot(qf[:, lanes], carried_in)
        factor = lax.rsqrt(jnp.mean(attn * attn, axis=1, keepdims=True) + 1e-06)
        scaled = attn * factor
        unit[:, lanes] = scaled
        scale[number] = jnp.broadcast_to(factor, (ROWS, DH))
        normed[:, lanes] = scaled.astype(BF)
        normed_t[lanes_of(number), :] = scaled.T.astype(BF)
        return 0

    lax.fori_loop(0, HEADS, finish_attention, 0)

    sib_down.wait_recv()
    add_gunit(other(down))
    sib_up.wait_recv()
    add_gunit(other(up))
    pass_top.wait_recv()
    pass_bottom.wait_recv()
    sib_across = links.start(whole(across), whole(across), sibling)
    add_gunit(block_of(across))
    sib_across.wait_recv()
    add_gunit(other(across))

    def weight_x(block, _):
        part = dot(normed_t[0:half, :], og[block]).astype(BF)
        for j in range(4):
            gx[block * 4 + j] = part[:, j * DH : (j + 1) * DH]
        return 0

    def weight_z(block, _):
        part = dot(normed_t[half:ROWS, :], og[block]).astype(BF)
        for j in range(4):
            gz[(lax.rem(block, 2) * 4 + j) * NX + block // 2] = part[:, j * DH : (j + 1) * DH]
        return 0

    ring_x = Ring(links, NX, x, at_x, lambda to: gx.at[pl.ds(to * NZ, NZ)], gx_half, gx_block)
    ring_z = Ring(links, NZ, z, at_z, lambda to: gz.at[pl.ds(to * NX, NX)], gz_half, gz_block)
    lax.fori_loop(0, 8, weight_x, 0)
    ring_x.begin()
    lax.fori_loop(0, 8, weight_z, 0)
    ring_z.begin()

    def grad_attn(number, _):
        lanes = lanes_of(number)
        given, scaled = gunit[:, lanes], unit[:, lanes]
        inner = jnp.mean(given * scaled, axis=1, keepdims=True)
        grad = (scale[number] * (given - scaled * inner)).astype(BF)
        go[:, lanes] = grad
        queries = (qf[:, lanes].astype(F32) * mask_head[...]).astype(BF)
        local = dot(queries, grad, 0, 0)
        bwd_send[pl.ds(2 * number, 2)] = local.astype(BF).reshape(2, DH // 2, DH)
        return 0

    lax.fori_loop(0, HEADS, grad_attn, 0)
    bwd_copies = to_owners(bwd_send, bwd_in)
    bwd_in[z] = bwd_send[z]

    ring_y = Ring(links, NY, y, at_y, lambda to: mix.at[to], mix_half, mix_block)
    order = [across, up, down, y]

    def project(block, put):
        columns = pl.ds(pl.multiple_of(block * WIDTH, WIDTH), WIDTH)

        def tile(r, _):
            rows = pl.ds(pl.multiple_of(r * half, half), half)
            put(r, dot(normed[rows, :], weight[:, columns]))
            return 0

        lax.fori_loop(0, 2, tile, 0)

    sib_copies = []
    for k, to in enumerate(order):

        def put_sib(r, part, k=k):
            sib_send[k, r] = part.astype(BF)

        project(other(to), put_sib)
        sib_copies.append(links.start(sib_send.at[k], sib_recv.at[k], sibling))

    def put_own(k, to):
        sib_copies[k].wait_recv()

        def put(r, part):
            mix[to, r] = (part + sib_recv[k, r].astype(F32)).astype(BF)

        project(block_of(to), put)

    for k, to in enumerate(order[:3]):
        put_own(k, to)
    ring_y.begin()
    put_own(3, y)

    ring_z.relay(2)

    for copy in bwd_copies:
        copy.wait_recv()
    run = jnp.zeros((DH // 2, DH), F32)
    suffix = [None] * NZ
    for k in range(NZ - 1, -1, -1):
        suffix[k] = run
        run = bwd_in[k].astype(F32) + same(k, k + 1) * run
    bwd_row[...] = run.astype(BF)
    back_copy = links.start(bwd_row, bwd_rowin, at_x(wrap(x - 1, NX)))

    def backward_local(number, _):
        lanes = lanes_of(number)
        for r in range(ROWS // DH):
            rows, width = slice(r * DH, (r + 1) * DH), (r + 1) * DH
            scores = dot(go[rows, lanes], val[0:width, lanes], 1, 1)
            kept = (scores * allowed[rows, 0:width]).astype(BF)
            gprobs[rows, 0:width] = kept
            gacts[0, rows, lanes] = dot(kept, kf[0:width, lanes])
        for r in range(ROWS // DH):
            rows, below = slice(r * DH, (r + 1) * DH), slice(r * DH, ROWS)
            gacts[1, rows, lanes] = dot(gprobs[below, rows], qf[below, lanes], 0, 0)
            gacts[2, rows, lanes] = dot(probs[number, below, rows], go[below, lanes], 0, 0)
        return 0

    back_copy.wait_recv()
    carried = bwd_rowin[...].astype(F32)
    for k in range(NZ):
        bwd_out[k] = (suffix[k] + same(k + 1, NZ) * carried).astype(BF)
    gout_copies = to_owners(bwd_out, gstate)
    gstate[z] = bwd_out[z]

    ring_x.relay(2)
    lax.fori_loop(0, HEADS, backward_local, 0)
    ring_z.relay(3)
    ring_y.relay(2)

    for copy in gout_copies:
        copy.wait_recv()

    def backward_state(number, _):
        lanes = lanes_of(number)
        carried_in = state[pl.ds(2 * number, 2)].reshape(DH, DH)
        carried_out = gstate[pl.ds(2 * number, 2)].reshape(DH, DH)
        queries, keys, values = qf[:, lanes], kf[:, lanes], val[:, lanes]
        slope = jnp.minimum(queries.astype(F32), 1.0)
        back = mask_head[...] * dot(go[:, lanes], carried_in, 1, 1)
        gacts[0, :, lanes] = (gacts[0, :, lanes] + back) * slope
        slope = jnp.minimum(keys.astype(F32), 1.0)
        back = mask_tail[...] * dot(values, carried_out, 1, 1)
        gacts[1, :, lanes] = (gacts[1, :, lanes] + back) * slope
        back = mask_tail[...] * dot(keys, carried_out)
        gacts[2, :, lanes] = gacts[2, :, lanes] + back
        return 0

    lax.fori_loop(0, HEADS, backward_state, 0)
    grim_copy = links.start(gacts.at[:, pl.ds(0, 8)], grim, token_prev)
    ring_z.relay(4)

    def unconvolve(number, _):
        lanes = lanes_of(number)
        for stream in range(3):
            grad = gacts[stream, :, lanes]
            raw = proj[stream, :, lanes].astype(F32)
            both = jnp.concatenate([rim[stream, :, lanes].astype(F32), raw], axis=0)
            acc = taps[stream, 0:1, lanes] * grad
            row = 4 * stream
            tap_part[row : row + 1, lanes] = jnp.sum(grad * raw, axis=0, keepdims=True)
            for j in range(1, KW):
                acc = acc + taps[stream, j : j + 1, lanes] * (
                    pltpu.roll(grad, ROWS - j, 0) * mask_next[j - 1]
                )
                lagged = pltpu.roll(both, j, 0)[EDGE:]
                tap_part[row + j : row + j + 1, lanes] = jnp.sum(
                    grad * mask_back[j - 1] * lagged, axis=0, keepdims=True
                )
            gproj_out[stream, :, lanes] = acc.astype(BF)
        return 0

    tap_part[12:16, :] = jnp.zeros((4, WIDTH), F32)
    lax.fori_loop(0, HEADS, unconvolve, 0)
    tap_copies = [
        links.start(tap_part, tap_in.at[z], at_z(wrap(z + k, NZ))) for k in range(1, NZ)
    ]
    tap_in[z] = tap_part[...]

    grim_copy.wait_recv()

    def unconvolve_rim(number, _):
        lanes = lanes_of(number)
        for stream in range(3):
            grad = gacts[stream, ROWS - EDGE : ROWS, lanes]
            both = jnp.concatenate([grad, grim[stream, :, lanes]], axis=0)
            acc = taps[stream, 0:1, lanes] * grad
            for j in range(1, KW):
                acc = acc + taps[stream, j : j + 1, lanes] * (
                    pltpu.roll(both, EDGE + 8 - j, 0)[0:EDGE]
                    * mask_next[j - 1, ROWS - EDGE : ROWS]
                )
            gproj_out[stream, ROWS - EDGE : ROWS, lanes] = acc.astype(BF)
        return 0

    lax.fori_loop(0, HEADS, unconvolve_rim, 0)

    for copy in tap_copies:
        copy.wait_recv()
    summed = tap_in[0]
    for k in range(1, NZ):
        summed = summed + tap_in[k]
    tap_row[...] = summed
    row_copies = [
        links.start(tap_row, tap_rowin.at[x], at_x(wrap(x + k, NX))) for k in range(1, NX)
    ]
    tap_rowin[x] = tap_row[...]

    ring_x2 = Ring(links, NZ, z, at_z, lambda to: gx2.at[to], gx2_half, gx2_block)
    ring_z2 = Ring(links, NX, x, at_x, lambda to: gz2.at[to], gz2_half, gz2_block)

    def second(ring, target):
        own, first, last = ring.finish()
        for k in range(own.shape[0]):
            value = own[k].astype(F32) + first[k].astype(F32) + last[k].astype(F32)
            target[k] = value.astype(BF).reshape(2, DH, DH)

    second(ring_x, gx2)
    ring_x2.begin()
    second(ring_z, gz2)
    ring_z2.begin()
    ring_x2.relay(2)
    ring_z2.relay(2)
    ring_x2.relay(3)

    own, first, last = ring_y.finish()
    for r in range(2):
        value = own[r].astype(F32) + first[r].astype(F32) + last[r].astype(F32)
        mixed_out[r * half : (r + 1) * half, :] = value.astype(BF)
    ring_x2.relay(4)

    for copy in row_copies:
        copy.wait_recv()
    summed = tap_rowin[0]
    for k in range(1, NX):
        summed = summed + tap_rowin[k]
    for stream in range(3):
        gtaps_out[stream] = summed[4 * stream : 4 * stream + 4, :]

    for ring, base in ((ring_z2, half), (ring_x2, 0)):
        own, first, last = ring.finish()
        for r in range(2):
            value = own[r].astype(F32) + first[r].astype(F32) + last[r].astype(F32)
            gweight_out[base + r * DH : base + (r + 1) * DH, :] = value
    links.drain()


def body(projected, conv_weight, out_weight, out_grad, doc_lengths):
    vm = lambda *shape: pltpu.VMEM(shape, BF)
    vf = lambda *shape: pltpu.VMEM(shape, F32)
    piece = (DH // 2, DH)
    hops = lambda n, m, *tile: [vm(2, m // 2, *tile), vm(2, n // 2 - 1, m, *tile)]
    carry = [vm(NZ, *piece), vm(NZ, *piece), vm(*piece), vm(*piece), vm(NZ, *piece), vm(NZ, *piece)]
    scratch = [
        vm(3, ROWS, WIDTH), vm(WIDTH, 8 * WIDTH), vm(8, ROWS, WIDTH), vm(3, EDGE, WIDTH), vf(3, 8, WIDTH),
        vf(3, ROWS, DH), vf(3, ROWS, DH), vf(ROWS, DH), vf(ROWS, DH), vf(ROWS, ROWS),
        vm(ROWS, WIDTH), vm(ROWS, WIDTH), vm(ROWS, WIDTH), vm(HEADS, ROWS, ROWS), vf(ROWS, WIDTH),
        vf(HEADS, ROWS, DH), vf(ROWS, WIDTH), vm(ROWS, WIDTH), vm(WIDTH, ROWS), vm(ROWS, WIDTH),
        vm(ROWS, ROWS), vf(3, ROWS, WIDTH),
        *carry, *carry,
        vm(4, 2, 256, WIDTH), vm(4, 2, 256, WIDTH), vm(4, 2, 256, WIDTH), *hops(NY, 2, 256, WIDTH),
        vm(32, 256, DH), *hops(NX, NZ, 256, DH), vm(NZ, 2, DH, DH), *hops(NZ, 2, DH, DH),
        vm(32, 256, DH), *hops(NZ, NX, 256, DH), vm(NX, 2, DH, DH), *hops(NX, 2, DH, DH),
        vf(16, WIDTH), vf(NZ, 16, WIDTH), vf(16, WIDTH), vf(NX, 16, WIDTH),
        pltpu.SemaphoreType.DMA((3,)), pltpu.SemaphoreType.DMA((COPIES,)), pltpu.SemaphoreType.DMA((COPIES,)),
    ]
    vmem = pl.BlockSpec(memory_space=pltpu.VMEM)
    outside = pl.BlockSpec(memory_space=pl.ANY)
    mixed, grad_projected, grad_conv, grad_out_weight = pl.pallas_call(
        kernel,
        out_shape=(
            jax.ShapeDtypeStruct((ROWS, WIDTH), BF),
            jax.ShapeDtypeStruct((3, ROWS, WIDTH), BF),
            jax.ShapeDtypeStruct((3, KW, WIDTH), F32),
            jax.ShapeDtypeStruct((WIDTH, DH), F32),
        ),
        in_specs=[pl.BlockSpec(memory_space=pltpu.SMEM), outside, vmem, outside, outside],
        out_specs=(vmem, vmem, vmem, vmem),
        scratch_shapes=scratch,
        compiler_params=pltpu.CompilerParams(
            collective_id=0, has_side_effects=True, vmem_limit_bytes=58 * 2**20
        ),
        cost_estimate=pl.CostEstimate(
            flops=8 * 10**9, bytes_accessed=10**7, transcendentals=10**6
        ),
    )(doc_lengths, projected, conv_weight, out_weight, out_grad)
    return mixed, grad_projected, grad_conv, grad_out_weight


def solution(mesh):
    return jax.shard_map(
        body,
        mesh=mesh,
        in_specs=(
            P(None, "seq", "head"),
            P(None, None, "head"),
            P("head", None),
            P("seq", "head"),
            P(),
        ),
        out_specs=(
            P("seq", "head"),
            P(None, "seq", "head"),
            P(None, None, "head"),
            P("head", "seq"),
        ),
        check_vma=False,
    )
```

```python
import jax
import jax.numpy as jnp
from jax import lax
from jax.experimental import pallas as pl
from jax.experimental.pallas import tpu as pltpu
from jax.sharding import PartitionSpec as P

DH = 128
KW = 4
HEADS = 4
ROWS = 512
WIDTH = 512
DOCS = 8
TOKENS = 16384
NX, NZ, NY = 4, 8, 4
EDGE = 16
BF = jnp.bfloat16
F32 = jnp.float32
MESH = pl.DeviceIdType.MESH
COPIES = 144
ZROWS = 256
XROWS = WIDTH - ZROWS


def wrap(value, size):
    return lax.rem(value + size, size)


def lanes_of(head):
    return pl.ds(pl.multiple_of(head * DH, DH), DH)


def dot(a, b, left=1, right=0):
    return lax.dot_general(a, b, (((left,), (right,)), ((), ())), preferred_element_type=F32)


class Links:
    def __init__(self, send_sems, recv_sems):
        self.send_sems, self.recv_sems = send_sems, recv_sems
        self.used, self.pending = 0, []

    def start(self, source, target, device):
        copy = pltpu.make_async_remote_copy(
            src_ref=source,
            dst_ref=target,
            send_sem=self.send_sems.at[self.used],
            recv_sem=self.recv_sems.at[self.used],
            device_id=device,
            device_id_type=MESH,
        )
        self.used += 1
        copy.start()
        self.pending.append(copy)
        return copy

    def drain(self):
        for copy in self.pending:
            copy.wait_send()


def add_into(target, source):
    for tile in range(target.shape[0]):
        target[tile] = (target[tile].astype(F32) + source[tile].astype(F32)).astype(BF)


class Ring:
    def __init__(self, links, n, me, device_of, own, halves, blocks):
        self.links, self.n, self.me = links, n, me
        self.device_of, self.own = device_of, own
        self.halves, self.blocks = halves, blocks
        self.arrivals = {}

    def part(self, way, ref, near):
        half = ref.shape[0] // 2
        first = (way == 0) == near
        return ref.at[pl.ds(0 if first else half, half)]

    def begin(self):
        far = self.n // 2
        for way, sign in ((0, 1), (1, -1)):
            there = self.device_of(wrap(self.me + sign, self.n))
            block = self.own(wrap(self.me + far, self.n))
            self.arrivals[way, 1] = [
                self.links.start(self.part(way, block, True), self.halves.at[way], there)
            ]
        for way, sign in ((0, 1), (1, -1)):
            there = self.device_of(wrap(self.me + sign, self.n))
            block = self.own(wrap(self.me + sign * (far - 1), self.n))
            self.arrivals[way, 2] = [
                self.links.start(
                    self.part(way, block, False),
                    self.part(way, self.blocks.at[way, 0], False),
                    there,
                )
            ]

    def relay(self, step):
        far = self.n // 2
        for way, sign in ((0, 1), (1, -1)):
            there = self.device_of(wrap(self.me + sign, self.n))
            block = self.own(wrap(self.me + sign * (far - step + 1), self.n))
            for copy in self.arrivals[way, step - 1]:
                copy.wait_recv()
            if step == 2:
                mine = self.part(way, block, True)
                add_into(mine, self.halves.at[way])
                landing = self.part(way, self.blocks.at[way, 0], True)
                self.arrivals[way, 2].append(self.links.start(mine, landing, there))
            else:
                add_into(block, self.blocks.at[way, step - 3])
                landing = self.blocks.at[way, step - 2]
                self.arrivals[way, step] = [self.links.start(block, landing, there)]

    def finish(self):
        last = self.n // 2
        for way in (0, 1):
            for copy in self.arrivals[way, last]:
                copy.wait_recv()
        return self.own(self.me), self.blocks.at[0, last - 2], self.blocks.at[1, last - 2]


def kernel(
    docs, proj_hbm, taps, weight_hbm, grad_hbm,
    mixed_out, gproj_out, gtaps_out, gweight_out,
    proj, weight, og, rim, grim,
    mask_back, mask_next, mask_head, mask_tail, allowed,
    qf, kf, val, probs, unit, scale, gunit, normed, normed_t, go, gprobs, gacts,
    fwd_send, fwd_in, fwd_row, fwd_rowin, fwd_out, state,
    bwd_send, bwd_in, bwd_row, bwd_rowin, bwd_out, gstate,
    sib_send, sib_recv, mix, mix_half, mix_block,
    gx, gx_half, gx_block, gx2, gx2_half, gx2_block,
    gz, gz_half, gz_block, gz2, gz2_half, gz2_block,
    tap_part, tap_send, tap_in, tap_row, tap_rowin,
    local_sems, send_sems, recv_sems,
):
    seq, head = lax.axis_index("seq"), lax.axis_index("head")
    x, z = seq // NZ, lax.rem(seq, NZ)
    y, core = head // 2, lax.rem(head, 2)
    at_x = lambda to: (to * NZ + z, head)
    at_z = lambda to: (x * NZ + to, head)
    at_y = lambda to: (seq, to * 2 + core)
    sibling = (seq, y * 2 + (1 - core))
    token_next = (wrap(seq + 1, NX * NZ), head)
    token_prev = (wrap(seq - 1, NX * NZ), head)
    links = Links(send_sems, recv_sems)

    partners = [sibling, at_y(wrap(y + 1, NY)), at_y(wrap(y - 1, NY)), token_next, token_prev]
    partners += [at_x(wrap(x + k, NX)) for k in range(1, NX)]
    partners += [at_z(wrap(z + k, NZ)) for k in range(1, NZ)]
    barrier = pltpu.get_barrier_semaphore()
    for partner in partners:
        pl.semaphore_signal(barrier, inc=1, device_id=partner, device_id_type=MESH)
    load_proj = pltpu.make_async_copy(proj_hbm, proj, local_sems.at[0])
    load_grad = pltpu.make_async_copy(grad_hbm, og.at[head], local_sems.at[1])
    load_weight = pltpu.make_async_copy(weight_hbm, weight, local_sems.at[2])
    load_proj.start()
    load_grad.start()
    load_weight.start()
    pl.semaphore_wait(barrier, len(partners))

    half = ROWS // 2
    up, down, across = wrap(y + 1, NY), wrap(y - 1, NY), wrap(y + 2, NY)
    block_of = lambda to: to * 2 + core
    upper, lower = pl.ds(0, half), pl.ds(half, half)
    top = lambda to: og.at[block_of(to), upper]
    bottom = lambda to: og.at[block_of(to), lower]
    whole = lambda to: og.at[block_of(to)]
    up_top = links.start(grad_hbm.at[upper], top(y), at_y(up))
    down_bottom = links.start(grad_hbm.at[lower], bottom(y), at_y(down))
    rim_copy = links.start(proj_hbm.at[:, pl.ds(ROWS - EDGE, EDGE)], rim, token_next)
    up_bottom = links.start(grad_hbm.at[lower], bottom(y), at_y(up))
    down_top = links.start(grad_hbm.at[upper], top(y), at_y(down))
    sib_own = links.start(grad_hbm, whole(y), sibling)

    starts = []
    total = jnp.int32(0)
    for i in range(DOCS):
        starts.append(total)
        total = total + docs[i]
    offset = seq * ROWS

    def doc_at(position):
        count = jnp.int32(0)
        for start in starts:
            count = count + jnp.where(start <= position, 1, 0)
        return count

    ends = [doc_at((x * NZ + k) * ROWS - 1) for k in range(NZ + 1)]
    same = lambda a, b: jnp.where(ends[a] == ends[b], jnp.float32(1), jnp.float32(0))

    position = offset + lax.broadcasted_iota(jnp.int32, (ROWS, DH), 0)
    doc_start = jnp.zeros((ROWS, DH), jnp.int32)
    doc_end = jnp.full((ROWS, DH), TOKENS, jnp.int32)
    for i in range(1, DOCS):
        doc_start = jnp.where(starts[i] <= position, starts[i], doc_start)
    for i in range(DOCS - 1, 0, -1):
        doc_end = jnp.where(starts[i] > position, starts[i], doc_end)
    one, zero = jnp.float32(1), jnp.float32(0)
    for j in range(1, KW):
        mask_back[j - 1] = jnp.where(position - j >= doc_start, one, zero)
        mask_next[j - 1] = jnp.where(position + j < doc_end, one, zero)
    mask_head[...] = jnp.where(doc_start < offset, one, zero)
    mask_tail[...] = jnp.where(doc_end > offset + ROWS - 1, one, zero)
    for tile in range(ROWS // DH):
        column = offset + tile * DH + lax.broadcasted_iota(jnp.int32, (ROWS, DH), 1)
        allowed[:, tile * DH : (tile + 1) * DH] = jnp.where(
            (column <= position) & (column >= doc_start), one, zero
        )

    load_proj.wait()

    def activate(stream, acc, rows, lanes):
        act = acc.astype(BF)
        if stream == 2:
            val[rows, lanes] = act
        else:
            wide = act.astype(F32)
            feature = jnp.where(wide > 0, wide + 1.0, jnp.exp(jnp.minimum(wide, 0.0)))
            (qf, kf)[stream][rows, lanes] = feature.astype(BF)

    def convolve(number, _):
        lanes = lanes_of(number)
        for stream in range(3):
            raw = proj[stream, :, lanes].astype(F32)
            acc = taps[stream, 0:1, lanes] * raw
            for j in range(1, KW):
                acc = acc + taps[stream, j : j + 1, lanes] * (
                    pltpu.roll(raw, j, 0) * mask_back[j - 1]
                )
            activate(stream, acc, slice(None), lanes)
        return 0

    lax.fori_loop(0, HEADS, convolve, 0)
    rim_copy.wait_recv()

    def convolve_rim(number, _):
        lanes = lanes_of(number)
        for stream in range(3):
            raw = proj[stream, 0:EDGE, lanes].astype(F32)
            both = jnp.concatenate([rim[stream, :, lanes].astype(F32), raw], axis=0)
            acc = taps[stream, 0:1, lanes] * raw
            for j in range(1, KW):
                acc = acc + taps[stream, j : j + 1, lanes] * (
                    pltpu.roll(both, j, 0)[EDGE:] * mask_back[j - 1, 0:EDGE]
                )
            activate(stream, acc, slice(0, EDGE), lanes)
        return 0

    lax.fori_loop(0, HEADS, convolve_rim, 0)

    def tail_state(number, _):
        lanes = lanes_of(number)
        keys = (kf[:, lanes].astype(F32) * mask_tail[...]).astype(BF)
        local = dot(keys, val[:, lanes], 0, 0)
        fwd_send[pl.ds(2 * number, 2)] = local.astype(BF).reshape(2, DH // 2, DH)
        return 0

    def to_owners(send, landing):
        return [
            links.start(send.at[wrap(z + k, NZ)], landing.at[z], at_z(wrap(z + k, NZ)))
            for k in range(1, NZ)
        ]

    lax.fori_loop(0, HEADS, tail_state, 0)
    fwd_copies = to_owners(fwd_send, fwd_in)
    fwd_in[z] = fwd_send[z]

    up_top.wait_recv()
    pass_top = links.start(top(down), top(down), at_y(up))
    down_bottom.wait_recv()
    pass_bottom = links.start(bottom(up), bottom(up), at_y(down))

    def local_attention(number, _):
        lanes = lanes_of(number)
        for r in range(ROWS // DH):
            rows, width = slice(r * DH, (r + 1) * DH), (r + 1) * DH
            scores = dot(qf[rows, lanes], kf[0:width, lanes], 1, 1)
            kept = (scores * allowed[rows, 0:width]).astype(BF)
            probs[number, rows, 0:width] = kept
            unit[rows, lanes] = dot(kept, val[0:width, lanes])
        return 0

    lax.fori_loop(0, HEADS, local_attention, 0)

    for copy in fwd_copies:
        copy.wait_recv()
    run = jnp.zeros((DH // 2, DH), F32)
    prefix = []
    for k in range(NZ):
        prefix.append(run)
        run = fwd_in[k].astype(F32) + same(k, k + 1) * run
    fwd_row[...] = run.astype(BF)
    row_copy = links.start(fwd_row, fwd_rowin, at_x(wrap(x + 1, NX)))

    load_grad.wait()
    load_weight.wait()

    def add_gunit(block, first=False):
        columns = pl.ds(pl.multiple_of(block * WIDTH, WIDTH), WIDTH)

        def tile(r, _):
            rows = pl.ds(pl.multiple_of(r * 256, 256), 256)
            part = dot(og[block, rows, :], weight[:, columns], 1, 1)
            gunit[rows, :] = part if first else gunit[rows, :] + part
            return 0

        lax.fori_loop(0, ROWS // 256, tile, 0)

    add_gunit(block_of(y), True)
    row_copy.wait_recv()
    carried = fwd_rowin[...].astype(F32)
    for k in range(NZ):
        fwd_out[k] = (prefix[k] + same(k, 0) * carried).astype(BF)
    out_copies = to_owners(fwd_out, state)
    state[z] = fwd_out[z]

    other = lambda to: to * 2 + (1 - core)
    sib_own.wait_recv()
    add_gunit(other(y))
    up_bottom.wait_recv()
    sib_down = links.start(whole(down), whole(down), sibling)
    down_top.wait_recv()
    sib_up = links.start(whole(up), whole(up), sibling)
    add_gunit(block_of(down))
    add_gunit(block_of(up))

    for copy in out_copies:
        copy.wait_recv()

    def finish_attention(number, _):
        lanes = lanes_of(number)
        carried_in = state[pl.ds(2 * number, 2)].reshape(DH, DH)
        attn = unit[:, lanes] + mask_head[...] * dot(qf[:, lanes], carried_in)
        factor = lax.rsqrt(jnp.mean(attn * attn, axis=1, keepdims=True) + 1e-06)
        scaled = attn * factor
        unit[:, lanes] = scaled
        scale[number] = jnp.broadcast_to(factor, (ROWS, DH))
        normed[:, lanes] = scaled.astype(BF)
        normed_t[lanes_of(number), :] = scaled.T.astype(BF)
        return 0

    lax.fori_loop(0, HEADS, finish_attention, 0)

    def weight_band(band):
        def one_block(which, _):
            block = band * 2 + which
            part = dot(normed_t[0:XROWS, :], og[block]).astype(BF)
            for j in range(4):
                gx[block * 4 + j] = part[:, j * DH : (j + 1) * DH]
            part = dot(normed_t[XROWS:WIDTH, :], og[block]).astype(BF)
            for j in range(4):
                tile = part[:, j * DH : (j + 1) * DH]
                gz[band, which * 4 + j] = tile.reshape(2, ZROWS // 2, DH)
            return 0

        lax.fori_loop(0, 2, one_block, 0)

    ring_x = Ring(links, NX, x, at_x, lambda to: gx.at[pl.ds(to * NZ, NZ)], gx_half, gx_block)
    order = [y, down, up, across]
    rings_z = [
        Ring(links, NZ, z, at_z, lambda to, b=b: gz.at[b, to], gz_half.at[k], gz_block.at[k])
        for k, b in enumerate(order)
    ]
    weight_band(y)
    rings_z[0].begin()
    sib_down.wait_recv()
    add_gunit(other(down))
    sib_up.wait_recv()
    add_gunit(other(up))
    pass_top.wait_recv()
    pass_bottom.wait_recv()
    sib_across = links.start(whole(across), whole(across), sibling)
    weight_band(down)
    rings_z[1].begin()
    weight_band(up)
    rings_z[2].begin()
    add_gunit(block_of(across))
    sib_across.wait_recv()
    add_gunit(other(across))
    weight_band(across)
    ring_x.begin()
    rings_z[3].begin()

    def grad_attn(number, _):
        lanes = lanes_of(number)
        given, scaled = gunit[:, lanes], unit[:, lanes]
        inner = jnp.mean(given * scaled, axis=1, keepdims=True)
        grad = (scale[number] * (given - scaled * inner)).astype(BF)
        go[:, lanes] = grad
        queries = (qf[:, lanes].astype(F32) * mask_head[...]).astype(BF)
        local = dot(queries, grad, 0, 0)
        bwd_send[pl.ds(2 * number, 2)] = local.astype(BF).reshape(2, DH // 2, DH)
        return 0

    lax.fori_loop(0, HEADS, grad_attn, 0)
    bwd_copies = to_owners(bwd_send, bwd_in)
    bwd_in[z] = bwd_send[z]
    rings_z[0].relay(2)

    ring_y = Ring(links, NY, y, at_y, lambda to: mix.at[to], mix_half, mix_block)
    outward = [across, up, down]

    def project(block, put):
        columns = pl.ds(pl.multiple_of(block * WIDTH, WIDTH), WIDTH)

        def tile(r, _):
            rows = pl.ds(pl.multiple_of(r * half, half), half)
            put(r, dot(normed[rows, :], weight[:, columns]))
            return 0

        lax.fori_loop(0, 2, tile, 0)

    sib_copies = []
    for k, to in enumerate(outward + [y]):

        def put_sib(r, part, k=k):
            sib_send[k, r] = part.astype(BF)

        project(other(to), put_sib)
        sib_copies.append(links.start(sib_send.at[k], sib_recv.at[k], sibling))

    def put_own(k, to):
        sib_copies[k].wait_recv()

        def put(r, part):
            mix[to, r] = (part + sib_recv[k, r].astype(F32)).astype(BF)

        project(block_of(to), put)

    rings_z[1].relay(2)
    rings_z[2].relay(2)
    rings_z[0].relay(3)

    for copy in bwd_copies:
        copy.wait_recv()
    run = jnp.zeros((DH // 2, DH), F32)
    suffix = [None] * NZ
    for k in range(NZ - 1, -1, -1):
        suffix[k] = run
        run = bwd_in[k].astype(F32) + same(k, k + 1) * run
    bwd_row[...] = run.astype(BF)
    back_copy = links.start(bwd_row, bwd_rowin, at_x(wrap(x - 1, NX)))

    for k, to in enumerate(outward):
        put_own(k, to)
    ring_y.begin()
    rings_z[3].relay(2)
    rings_z[1].relay(3)
    rings_z[2].relay(3)
    rings_z[0].relay(4)
    ring_x.relay(2)

    def backward_local(number, _):
        lanes = lanes_of(number)
        for r in range(ROWS // DH):
            rows, width = slice(r * DH, (r + 1) * DH), (r + 1) * DH
            scores = dot(go[rows, lanes], val[0:width, lanes], 1, 1)
            kept = (scores * allowed[rows, 0:width]).astype(BF)
            gprobs[rows, 0:width] = kept
            gacts[0, rows, lanes] = dot(kept, kf[0:width, lanes])
        for r in range(ROWS // DH):
            rows, below = slice(r * DH, (r + 1) * DH), slice(r * DH, ROWS)
            gacts[1, rows, lanes] = dot(gprobs[below, rows], qf[below, lanes], 0, 0)
            gacts[2, rows, lanes] = dot(probs[number, below, rows], go[below, lanes], 0, 0)
        return 0

    back_copy.wait_recv()
    carried = bwd_rowin[...].astype(F32)
    for k in range(NZ):
        bwd_out[k] = (suffix[k] + same(k + 1, NZ) * carried).astype(BF)
    gout_copies = to_owners(bwd_out, gstate)
    gstate[z] = bwd_out[z]

    lax.fori_loop(0, HEADS, backward_local, 0)
    rings_z[3].relay(3)
    rings_z[1].relay(4)
    rings_z[2].relay(4)
    put_own(3, y)

    for copy in gout_copies:
        copy.wait_recv()

    def backward_state(number, _):
        lanes = lanes_of(number)
        carried_in = state[pl.ds(2 * number, 2)].reshape(DH, DH)
        carried_out = gstate[pl.ds(2 * number, 2)].reshape(DH, DH)
        queries, keys, values = qf[:, lanes], kf[:, lanes], val[:, lanes]
        slope = jnp.minimum(queries.astype(F32), 1.0)
        back = mask_head[...] * dot(go[:, lanes], carried_in, 1, 1)
        gacts[0, :, lanes] = (gacts[0, :, lanes] + back) * slope
        slope = jnp.minimum(keys.astype(F32), 1.0)
        back = mask_tail[...] * dot(values, carried_out, 1, 1)
        gacts[1, :, lanes] = (gacts[1, :, lanes] + back) * slope
        back = mask_tail[...] * dot(keys, carried_out)
        gacts[2, :, lanes] = gacts[2, :, lanes] + back
        return 0

    lax.fori_loop(0, HEADS, backward_state, 0)
    grim_copy = links.start(gacts.at[:, pl.ds(0, 8)], grim, token_prev)
    ring_y.relay(2)
    rings_z[3].relay(4)

    def unconvolve(number, _):
        lanes = lanes_of(number)
        for stream in range(3):
            grad = gacts[stream, :, lanes]
            raw = proj[stream, :, lanes].astype(F32)
            both = jnp.concatenate([rim[stream, :, lanes].astype(F32), raw], axis=0)
            acc = taps[stream, 0:1, lanes] * grad
            row = 4 * stream
            tap_part[row : row + 1, lanes] = jnp.sum(grad * raw, axis=0, keepdims=True)
            for j in range(1, KW):
                acc = acc + taps[stream, j : j + 1, lanes] * (
                    pltpu.roll(grad, ROWS - j, 0) * mask_next[j - 1]
                )
                lagged = pltpu.roll(both, j, 0)[EDGE:]
                tap_part[row + j : row + j + 1, lanes] = jnp.sum(
                    grad * mask_back[j - 1] * lagged, axis=0, keepdims=True
                )
            gproj_out[stream, :, lanes] = acc.astype(BF)
        return 0

    tap_part[12:16, :] = jnp.zeros((4, WIDTH), F32)
    lax.fori_loop(0, HEADS, unconvolve, 0)
    tap_send[...] = tap_part[...].astype(BF)
    tap_copies = [
        links.start(tap_send, tap_in.at[z], at_z(wrap(z + k, NZ))) for k in range(1, NZ)
    ]
    tap_in[z] = tap_send[...]

    grim_copy.wait_recv()

    def unconvolve_rim(number, _):
        lanes = lanes_of(number)
        for stream in range(3):
            grad = gacts[stream, ROWS - EDGE : ROWS, lanes]
            both = jnp.concatenate([grad, grim[stream, :, lanes]], axis=0)
            acc = taps[stream, 0:1, lanes] * grad
            for j in range(1, KW):
                acc = acc + taps[stream, j : j + 1, lanes] * (
                    pltpu.roll(both, EDGE + 8 - j, 0)[0:EDGE]
                    * mask_next[j - 1, ROWS - EDGE : ROWS]
                )
            gproj_out[stream, ROWS - EDGE : ROWS, lanes] = acc.astype(BF)
        return 0

    lax.fori_loop(0, HEADS, unconvolve_rim, 0)

    ring_x2 = Ring(links, NZ, z, at_z, lambda to: gx2.at[to], gx2_half, gx2_block)
    ring_z2 = Ring(links, NX, x, at_x, lambda to: gz2.at[to], gz2_half, gz2_block)

    for ring, band in zip(rings_z, order):
        own, first, last = ring.finish()
        for r in range(2):
            value = own[r].astype(F32) + first[r].astype(F32) + last[r].astype(F32)
            gz2[band, r] = value.astype(BF)
    ring_z2.begin()
    own, first, last = ring_x.finish()
    for k in range(NZ):
        value = own[k].astype(F32) + first[k].astype(F32) + last[k].astype(F32)
        gx2[k] = value.astype(BF).reshape(2, XROWS // 2, DH)
    ring_x2.begin()
    ring_z2.relay(2)

    for copy in tap_copies:
        copy.wait_recv()
    summed = tap_in[0].astype(F32)
    for k in range(1, NZ):
        summed = summed + tap_in[k].astype(F32)
    tap_row[...] = summed
    row_copies = [
        links.start(tap_row, tap_rowin.at[x], at_x(wrap(x + k, NX))) for k in range(1, NX)
    ]
    tap_rowin[x] = tap_row[...]
    ring_x2.relay(2)

    own, first, last = ring_y.finish()
    for r in range(2):
        value = own[r].astype(F32) + first[r].astype(F32) + last[r].astype(F32)
        mixed_out[r * half : (r + 1) * half, :] = value.astype(BF)
    ring_x2.relay(3)

    for copy in row_copies:
        copy.wait_recv()
    summed = tap_rowin[0]
    for k in range(1, NX):
        summed = summed + tap_rowin[k]
    for stream in range(3):
        gtaps_out[stream] = summed[4 * stream : 4 * stream + 4, :]
    ring_x2.relay(4)

    for ring, base, count in ((ring_z2, XROWS, ZROWS // 2), (ring_x2, 0, XROWS // 2)):
        own, first, last = ring.finish()
        for r in range(2):
            value = own[r].astype(F32) + first[r].astype(F32) + last[r].astype(F32)
            gweight_out[base + r * count : base + (r + 1) * count, :] = value
    links.drain()


def hand_over(*refs):
    sources, targets, sems = refs[:4], refs[4:8], refs[8]
    copies = [
        pltpu.make_async_copy(source, target, sems.at[k])
        for k, (source, target) in enumerate(zip(sources, targets))
    ]
    for copy in copies:
        copy.start()
    for copy in copies:
        copy.wait()


def body(projected, conv_weight, out_weight, out_grad, doc_lengths):
    vm = lambda *shape: pltpu.VMEM(shape, BF)
    vf = lambda *shape: pltpu.VMEM(shape, F32)
    piece = (DH // 2, DH)
    hops = lambda n, m, *tile: [vm(2, m // 2, *tile), vm(2, n // 2 - 1, m, *tile)]
    carry = [vm(NZ, *piece), vm(NZ, *piece), vm(*piece), vm(*piece), vm(NZ, *piece), vm(NZ, *piece)]
    scratch = [
        vm(3, ROWS, WIDTH), vm(WIDTH, 8 * WIDTH), vm(8, ROWS, WIDTH), vm(3, EDGE, WIDTH), vf(3, 8, WIDTH),
        vf(3, ROWS, DH), vf(3, ROWS, DH), vf(ROWS, DH), vf(ROWS, DH), vf(ROWS, ROWS),
        vm(ROWS, WIDTH), vm(ROWS, WIDTH), vm(ROWS, WIDTH), vm(HEADS, ROWS, ROWS), vf(ROWS, WIDTH),
        vf(HEADS, ROWS, DH), vf(ROWS, WIDTH), vm(ROWS, WIDTH), vm(WIDTH, ROWS), vm(ROWS, WIDTH),
        vm(ROWS, ROWS), vf(3, ROWS, WIDTH),
        *carry, *carry,
        vm(4, 2, 256, WIDTH), vm(4, 2, 256, WIDTH), vm(4, 2, 256, WIDTH), *hops(NY, 2, 256, WIDTH),
        vm(32, XROWS, DH), *hops(NX, NZ, XROWS, DH),
        vm(NZ, 2, XROWS // 2, DH), *hops(NZ, 2, XROWS // 2, DH),
        vm(NX, NZ, 2, ZROWS // 2, DH), vm(4, 2, 1, ZROWS // 2, DH), vm(4, 2, 3, 2, ZROWS // 2, DH),
        vm(NX, 2, ZROWS // 2, DH), *hops(NX, 2, ZROWS // 2, DH),
        vf(16, WIDTH), vm(16, WIDTH), vm(NZ, 16, WIDTH), vf(16, WIDTH), vf(NX, 16, WIDTH),
        pltpu.SemaphoreType.DMA((3,)), pltpu.SemaphoreType.DMA((COPIES,)), pltpu.SemaphoreType.DMA((COPIES,)),
    ]
    vmem = pl.BlockSpec(memory_space=pltpu.VMEM)
    outside = pl.BlockSpec(memory_space=pl.ANY)
    shapes = (
        jax.ShapeDtypeStruct((ROWS, WIDTH), BF),
        jax.ShapeDtypeStruct((3, ROWS, WIDTH), BF),
        jax.ShapeDtypeStruct((3, KW, WIDTH), F32),
        jax.ShapeDtypeStruct((WIDTH, DH), F32),
    )
    results = pl.pallas_call(
        kernel,
        out_shape=[pltpu.VMEM(shape.shape, shape.dtype) for shape in shapes],
        in_specs=[pl.BlockSpec(memory_space=pltpu.SMEM), outside, vmem, outside, outside],
        out_specs=[vmem] * 4,
        scratch_shapes=scratch,
        compiler_params=pltpu.CompilerParams(
            collective_id=0, has_side_effects=True, vmem_limit_bytes=58 * 2**20
        ),
        cost_estimate=pl.CostEstimate(
            flops=8 * 10**9, bytes_accessed=10**7, transcendentals=10**6
        ),
    )(doc_lengths, projected, conv_weight, out_weight, out_grad)
    return pl.pallas_call(
        hand_over,
        out_shape=shapes,
        in_specs=[outside] * 4,
        out_specs=(outside,) * 4,
        scratch_shapes=[pltpu.SemaphoreType.DMA((4,))],
        compiler_params=pltpu.CompilerParams(vmem_limit_bytes=2**20),
        cost_estimate=pl.CostEstimate(flops=0, bytes_accessed=5 * 10**6, transcendentals=0),
    )(*results)


def solution(mesh):
    return jax.shard_map(
        body,
        mesh=mesh,
        in_specs=(
            P(None, "seq", "head"),
            P(None, None, "head"),
            P("head", None),
            P("seq", "head"),
            P(),
        ),
        out_specs=(
            P("seq", "head"),
            P(None, "seq", "head"),
            P(None, None, "head"),
            P("head", "seq"),
        ),
        check_vma=False,
    )
```

```python
import jax
import jax.numpy as jnp
from jax import lax
from jax.experimental import pallas as pl
from jax.experimental.pallas import tpu as pltpu
from jax.sharding import PartitionSpec as P

DH = 128
KW = 4
HEADS = 4
ROWS = 512
WIDTH = 512
DOCS = 8
TOKENS = 16384
NX, NZ, NY = 4, 8, 4
EDGE = 16
BF = jnp.bfloat16
F32 = jnp.float32
MESH = pl.DeviceIdType.MESH
COPIES = 144
ZROWS = 256
XROWS = WIDTH - ZROWS


def wrap(value, size):
    return lax.rem(value + size, size)


def lanes_of(head):
    return pl.ds(pl.multiple_of(head * DH, DH), DH)


def dot(a, b, left=1, right=0):
    return lax.dot_general(a, b, (((left,), (right,)), ((), ())), preferred_element_type=F32)


class Links:
    def __init__(self, send_sems, recv_sems):
        self.send_sems, self.recv_sems = send_sems, recv_sems
        self.used, self.pending = 0, []

    def start(self, source, target, device):
        copy = pltpu.make_async_remote_copy(
            src_ref=source,
            dst_ref=target,
            send_sem=self.send_sems.at[self.used],
            recv_sem=self.recv_sems.at[self.used],
            device_id=device,
            device_id_type=MESH,
        )
        self.used += 1
        copy.start()
        self.pending.append(copy)
        return copy

    def drain(self):
        for copy in self.pending:
            copy.wait_send()


def add_into(target, source):
    for tile in range(target.shape[0]):
        target[tile] = (target[tile].astype(F32) + source[tile].astype(F32)).astype(BF)


class Ring:
    def __init__(self, links, n, me, device_of, own, halves, blocks):
        self.links, self.n, self.me = links, n, me
        self.device_of, self.own = device_of, own
        self.halves, self.blocks = halves, blocks
        self.arrivals = {}

    def part(self, way, ref, near):
        half = ref.shape[0] // 2
        first = (way == 0) == near
        return ref.at[pl.ds(0 if first else half, half)]

    def begin(self):
        far = self.n // 2
        for way, sign in ((0, 1), (1, -1)):
            there = self.device_of(wrap(self.me + sign, self.n))
            block = self.own(wrap(self.me + far, self.n))
            self.arrivals[way, 1] = [
                self.links.start(self.part(way, block, True), self.halves.at[way], there)
            ]
        for way, sign in ((0, 1), (1, -1)):
            there = self.device_of(wrap(self.me + sign, self.n))
            block = self.own(wrap(self.me + sign * (far - 1), self.n))
            self.arrivals[way, 2] = [
                self.links.start(
                    self.part(way, block, False),
                    self.part(way, self.blocks.at[way, 0], False),
                    there,
                )
            ]

    def relay(self, step):
        far = self.n // 2
        for way, sign in ((0, 1), (1, -1)):
            there = self.device_of(wrap(self.me + sign, self.n))
            block = self.own(wrap(self.me + sign * (far - step + 1), self.n))
            for copy in self.arrivals[way, step - 1]:
                copy.wait_recv()
            if step == 2:
                mine = self.part(way, block, True)
                add_into(mine, self.halves.at[way])
                landing = self.part(way, self.blocks.at[way, 0], True)
                self.arrivals[way, 2].append(self.links.start(mine, landing, there))
            else:
                add_into(block, self.blocks.at[way, step - 3])
                landing = self.blocks.at[way, step - 2]
                self.arrivals[way, step] = [self.links.start(block, landing, there)]

    def finish(self):
        last = self.n // 2
        for way in (0, 1):
            for copy in self.arrivals[way, last]:
                copy.wait_recv()
        return self.own(self.me), self.blocks.at[0, last - 2], self.blocks.at[1, last - 2]


def kernel(
    docs, proj_hbm, taps, weight_hbm, grad_hbm,
    mixed_out, gproj_out, gtaps_out, gweight_out,
    proj, weight, og, rim, grim,
    mask_back, mask_next, mask_head, mask_tail, allowed,
    qf, kf, val, probs, unit, scale, gunit, normed, normed_t, go, gprobs, gacts,
    fwd_send, fwd_in, fwd_row, fwd_rowin, fwd_out, state,
    bwd_send, bwd_in, bwd_row, bwd_rowin, bwd_out, gstate,
    sib_send, sib_recv, mix, mix_half, mix_block,
    gx, gx_half, gx_block, gx2, gx2_half, gx2_block,
    gz, gz_half, gz_block, gz2, gz2_half, gz2_block,
    tap_part, tap_send, tap_in, tap_row, tap_rowin,
    local_sems, send_sems, recv_sems,
):
    seq, head = lax.axis_index("seq"), lax.axis_index("head")
    x, z = seq // NZ, lax.rem(seq, NZ)
    y, core = head // 2, lax.rem(head, 2)
    at_x = lambda to: (to * NZ + z, head)
    at_z = lambda to: (x * NZ + to, head)
    at_y = lambda to: (seq, to * 2 + core)
    sibling = (seq, y * 2 + (1 - core))
    token_next = (wrap(seq + 1, NX * NZ), head)
    token_prev = (wrap(seq - 1, NX * NZ), head)
    links = Links(send_sems, recv_sems)

    partners = [sibling, at_y(wrap(y + 1, NY)), at_y(wrap(y - 1, NY)), token_next, token_prev]
    partners += [at_x(wrap(x + k, NX)) for k in range(1, NX)]
    partners += [at_z(wrap(z + k, NZ)) for k in range(1, NZ)]
    barrier = pltpu.get_barrier_semaphore()
    for partner in partners:
        pl.semaphore_signal(barrier, inc=1, device_id=partner, device_id_type=MESH)
    load_proj = pltpu.make_async_copy(proj_hbm, proj, local_sems.at[0])
    load_grad = pltpu.make_async_copy(grad_hbm, og.at[head], local_sems.at[1])
    load_weight = pltpu.make_async_copy(weight_hbm, weight, local_sems.at[2])
    load_proj.start()
    load_grad.start()
    load_weight.start()
    pl.semaphore_wait(barrier, len(partners))

    half = ROWS // 2
    up, down, across = wrap(y + 1, NY), wrap(y - 1, NY), wrap(y + 2, NY)
    block_of = lambda to: to * 2 + core
    upper, lower = pl.ds(0, half), pl.ds(half, half)
    top = lambda to: og.at[block_of(to), upper]
    bottom = lambda to: og.at[block_of(to), lower]
    whole = lambda to: og.at[block_of(to)]
    up_top = links.start(grad_hbm.at[upper], top(y), at_y(up))
    down_bottom = links.start(grad_hbm.at[lower], bottom(y), at_y(down))
    rim_copy = links.start(proj_hbm.at[:, pl.ds(ROWS - EDGE, EDGE)], rim, token_next)
    up_bottom = links.start(grad_hbm.at[lower], bottom(y), at_y(up))
    down_top = links.start(grad_hbm.at[upper], top(y), at_y(down))
    sib_own = links.start(grad_hbm, whole(y), sibling)

    starts = []
    total = jnp.int32(0)
    for i in range(DOCS):
        starts.append(total)
        total = total + docs[i]
    offset = seq * ROWS

    def doc_at(position):
        count = jnp.int32(0)
        for start in starts:
            count = count + jnp.where(start <= position, 1, 0)
        return count

    ends = [doc_at((x * NZ + k) * ROWS - 1) for k in range(NZ + 1)]
    same = lambda a, b: jnp.where(ends[a] == ends[b], jnp.float32(1), jnp.float32(0))

    position = offset + lax.broadcasted_iota(jnp.int32, (ROWS, DH), 0)
    doc_start = jnp.zeros((ROWS, DH), jnp.int32)
    doc_end = jnp.full((ROWS, DH), TOKENS, jnp.int32)
    for i in range(1, DOCS):
        doc_start = jnp.where(starts[i] <= position, starts[i], doc_start)
    for i in range(DOCS - 1, 0, -1):
        doc_end = jnp.where(starts[i] > position, starts[i], doc_end)
    one, zero = jnp.float32(1), jnp.float32(0)
    for j in range(1, KW):
        mask_back[j - 1] = jnp.where(position - j >= doc_start, one, zero)
        mask_next[j - 1] = jnp.where(position + j < doc_end, one, zero)
    mask_head[...] = jnp.where(doc_start < offset, one, zero)
    mask_tail[...] = jnp.where(doc_end > offset + ROWS - 1, one, zero)
    for tile in range(ROWS // DH):
        column = offset + tile * DH + lax.broadcasted_iota(jnp.int32, (ROWS, DH), 1)
        allowed[:, tile * DH : (tile + 1) * DH] = jnp.where(
            (column <= position) & (column >= doc_start), one, zero
        )

    load_proj.wait()

    def activate(stream, acc, rows, lanes):
        act = acc.astype(BF)
        if stream == 2:
            val[rows, lanes] = act
        else:
            wide = act.astype(F32)
            feature = jnp.where(wide > 0, wide + 1.0, jnp.exp(jnp.minimum(wide, 0.0)))
            (qf, kf)[stream][rows, lanes] = feature.astype(BF)

    def convolve(number, _):
        lanes = lanes_of(number)
        for stream in range(3):
            raw = proj[stream, :, lanes].astype(F32)
            acc = taps[stream, 0:1, lanes] * raw
            for j in range(1, KW):
                acc = acc + taps[stream, j : j + 1, lanes] * (
                    pltpu.roll(raw, j, 0) * mask_back[j - 1]
                )
            activate(stream, acc, slice(None), lanes)
        return 0

    lax.fori_loop(0, HEADS, convolve, 0, unroll=True)
    rim_copy.wait_recv()

    def convolve_rim(number, _):
        lanes = lanes_of(number)
        for stream in range(3):
            raw = proj[stream, 0:EDGE, lanes].astype(F32)
            both = jnp.concatenate([rim[stream, :, lanes].astype(F32), raw], axis=0)
            acc = taps[stream, 0:1, lanes] * raw
            for j in range(1, KW):
                acc = acc + taps[stream, j : j + 1, lanes] * (
                    pltpu.roll(both, j, 0)[EDGE:] * mask_back[j - 1, 0:EDGE]
                )
            activate(stream, acc, slice(0, EDGE), lanes)
        return 0

    lax.fori_loop(0, HEADS, convolve_rim, 0, unroll=True)

    def tail_state(number, _):
        lanes = lanes_of(number)
        keys = (kf[:, lanes].astype(F32) * mask_tail[...]).astype(BF)
        local = dot(keys, val[:, lanes], 0, 0)
        fwd_send[pl.ds(2 * number, 2)] = local.astype(BF).reshape(2, DH // 2, DH)
        return 0

    def to_owners(send, landing):
        return [
            links.start(send.at[wrap(z + k, NZ)], landing.at[z], at_z(wrap(z + k, NZ)))
            for k in range(1, NZ)
        ]

    lax.fori_loop(0, HEADS, tail_state, 0, unroll=True)
    fwd_copies = to_owners(fwd_send, fwd_in)
    fwd_in[z] = fwd_send[z]

    up_top.wait_recv()
    pass_top = links.start(top(down), top(down), at_y(up))
    down_bottom.wait_recv()
    pass_bottom = links.start(bottom(up), bottom(up), at_y(down))

    def local_attention(number, _):
        lanes = lanes_of(number)
        for r in range(ROWS // DH):
            rows, width = slice(r * DH, (r + 1) * DH), (r + 1) * DH
            scores = dot(qf[rows, lanes], kf[0:width, lanes], 1, 1)
            kept = (scores * allowed[rows, 0:width]).astype(BF)
            probs[number, rows, 0:width] = kept
            unit[rows, lanes] = dot(kept, val[0:width, lanes])
        return 0

    lax.fori_loop(0, HEADS, local_attention, 0, unroll=True)

    for copy in fwd_copies:
        copy.wait_recv()
    run = jnp.zeros((DH // 2, DH), F32)
    prefix = []
    for k in range(NZ):
        prefix.append(run)
        run = fwd_in[k].astype(F32) + same(k, k + 1) * run
    fwd_row[...] = run.astype(BF)
    row_copy = links.start(fwd_row, fwd_rowin, at_x(wrap(x + 1, NX)))

    load_grad.wait()
    load_weight.wait()

    def add_gunit(block, first=False):
        columns = pl.ds(pl.multiple_of(block * WIDTH, WIDTH), WIDTH)

        def tile(r, _):
            rows = pl.ds(pl.multiple_of(r * 256, 256), 256)
            part = dot(og[block, rows, :], weight[:, columns], 1, 1)
            gunit[rows, :] = part if first else gunit[rows, :] + part
            return 0

        lax.fori_loop(0, ROWS // 256, tile, 0, unroll=True)

    add_gunit(block_of(y), True)
    row_copy.wait_recv()
    carried = fwd_rowin[...].astype(F32)
    for k in range(NZ):
        fwd_out[k] = (prefix[k] + same(k, 0) * carried).astype(BF)
    out_copies = to_owners(fwd_out, state)
    state[z] = fwd_out[z]

    other = lambda to: to * 2 + (1 - core)
    sib_own.wait_recv()
    add_gunit(other(y))
    up_bottom.wait_recv()
    sib_down = links.start(whole(down), whole(down), sibling)
    down_top.wait_recv()
    sib_up = links.start(whole(up), whole(up), sibling)

    for copy in out_copies:
        copy.wait_recv()

    def finish_attention(number, _):
        lanes = lanes_of(number)
        carried_in = state[pl.ds(2 * number, 2)].reshape(DH, DH)
        attn = unit[:, lanes] + mask_head[...] * dot(qf[:, lanes], carried_in)
        factor = lax.rsqrt(jnp.mean(attn * attn, axis=1, keepdims=True) + 1e-06)
        scaled = attn * factor
        unit[:, lanes] = scaled
        scale[number] = jnp.broadcast_to(factor, (ROWS, DH))
        normed[:, lanes] = scaled.astype(BF)
        normed_t[lanes_of(number), :] = scaled.T.astype(BF)
        return 0

    lax.fori_loop(0, HEADS, finish_attention, 0, unroll=True)

    def weight_band(band):
        def one_block(which, _):
            block = band * 2 + which
            part = dot(normed_t[0:XROWS, :], og[block]).astype(BF)
            for j in range(4):
                gx[block * 4 + j] = part[:, j * DH : (j + 1) * DH]
            part = dot(normed_t[XROWS:WIDTH, :], og[block]).astype(BF)
            for j in range(4):
                tile = part[:, j * DH : (j + 1) * DH]
                gz[band, which * 4 + j] = tile.reshape(2, ZROWS // 2, DH)
            return 0

        lax.fori_loop(0, 2, one_block, 0, unroll=True)

    ring_x = Ring(links, NX, x, at_x, lambda to: gx.at[pl.ds(to * NZ, NZ)], gx_half, gx_block)
    order = [y, down, up, across]
    rings_z = [
        Ring(links, NZ, z, at_z, lambda to, b=b: gz.at[b, to], gz_half.at[k], gz_block.at[k])
        for k, b in enumerate(order)
    ]
    weight_band(y)
    rings_z[0].begin()
    add_gunit(block_of(down))
    add_gunit(block_of(up))
    sib_down.wait_recv()
    weight_band(down)
    rings_z[1].begin()
    pass_top.wait_recv()
    pass_bottom.wait_recv()
    sib_across = links.start(whole(across), whole(across), sibling)
    sib_up.wait_recv()
    weight_band(up)
    rings_z[2].begin()
    add_gunit(other(down))
    add_gunit(other(up))
    add_gunit(block_of(across))
    sib_across.wait_recv()
    add_gunit(other(across))
    weight_band(across)
    ring_x.begin()
    rings_z[3].begin()

    def grad_attn(number, _):
        lanes = lanes_of(number)
        given, scaled = gunit[:, lanes], unit[:, lanes]
        inner = jnp.mean(given * scaled, axis=1, keepdims=True)
        grad = (scale[number] * (given - scaled * inner)).astype(BF)
        go[:, lanes] = grad
        queries = (qf[:, lanes].astype(F32) * mask_head[...]).astype(BF)
        local = dot(queries, grad, 0, 0)
        bwd_send[pl.ds(2 * number, 2)] = local.astype(BF).reshape(2, DH // 2, DH)
        return 0

    lax.fori_loop(0, HEADS, grad_attn, 0, unroll=True)
    bwd_copies = to_owners(bwd_send, bwd_in)
    bwd_in[z] = bwd_send[z]
    rings_z[0].relay(2)

    ring_y = Ring(links, NY, y, at_y, lambda to: mix.at[to], mix_half, mix_block)
    outward = [across, up, down]

    def project(block, put):
        columns = pl.ds(pl.multiple_of(block * WIDTH, WIDTH), WIDTH)

        def tile(r, _):
            rows = pl.ds(pl.multiple_of(r * half, half), half)
            put(r, dot(normed[rows, :], weight[:, columns]))
            return 0

        lax.fori_loop(0, 2, tile, 0, unroll=True)

    sib_copies = []
    for k, to in enumerate(outward + [y]):

        def put_sib(r, part, k=k):
            sib_send[k, r] = part.astype(BF)

        project(other(to), put_sib)
        sib_copies.append(links.start(sib_send.at[k], sib_recv.at[k], sibling))

    def put_own(k, to):
        sib_copies[k].wait_recv()

        def put(r, part):
            mix[to, r] = (part + sib_recv[k, r].astype(F32)).astype(BF)

        project(block_of(to), put)

    rings_z[1].relay(2)
    rings_z[2].relay(2)
    rings_z[0].relay(3)

    for copy in bwd_copies:
        copy.wait_recv()
    run = jnp.zeros((DH // 2, DH), F32)
    suffix = [None] * NZ
    for k in range(NZ - 1, -1, -1):
        suffix[k] = run
        run = bwd_in[k].astype(F32) + same(k, k + 1) * run
    bwd_row[...] = run.astype(BF)
    back_copy = links.start(bwd_row, bwd_rowin, at_x(wrap(x - 1, NX)))

    for k, to in enumerate(outward):
        put_own(k, to)
    ring_y.begin()
    rings_z[3].relay(2)
    rings_z[1].relay(3)
    rings_z[2].relay(3)
    rings_z[0].relay(4)
    ring_x.relay(2)

    def backward_local(number, _):
        lanes = lanes_of(number)
        for r in range(ROWS // DH):
            rows, width = slice(r * DH, (r + 1) * DH), (r + 1) * DH
            scores = dot(go[rows, lanes], val[0:width, lanes], 1, 1)
            kept = (scores * allowed[rows, 0:width]).astype(BF)
            gprobs[rows, 0:width] = kept
            gacts[0, rows, lanes] = dot(kept, kf[0:width, lanes])
        for r in range(ROWS // DH):
            rows, below = slice(r * DH, (r + 1) * DH), slice(r * DH, ROWS)
            gacts[1, rows, lanes] = dot(gprobs[below, rows], qf[below, lanes], 0, 0)
            gacts[2, rows, lanes] = dot(probs[number, below, rows], go[below, lanes], 0, 0)
        return 0

    back_copy.wait_recv()
    carried = bwd_rowin[...].astype(F32)
    for k in range(NZ):
        bwd_out[k] = (suffix[k] + same(k + 1, NZ) * carried).astype(BF)
    gout_copies = to_owners(bwd_out, gstate)
    gstate[z] = bwd_out[z]

    lax.fori_loop(0, HEADS, backward_local, 0, unroll=True)
    rings_z[3].relay(3)
    rings_z[1].relay(4)
    rings_z[2].relay(4)
    put_own(3, y)

    for copy in gout_copies:
        copy.wait_recv()

    def backward_state(number, _):
        lanes = lanes_of(number)
        carried_in = state[pl.ds(2 * number, 2)].reshape(DH, DH)
        carried_out = gstate[pl.ds(2 * number, 2)].reshape(DH, DH)
        queries, keys, values = qf[:, lanes], kf[:, lanes], val[:, lanes]
        slope = jnp.minimum(queries.astype(F32), 1.0)
        back = mask_head[...] * dot(go[:, lanes], carried_in, 1, 1)
        gacts[0, :, lanes] = (gacts[0, :, lanes] + back) * slope
        slope = jnp.minimum(keys.astype(F32), 1.0)
        back = mask_tail[...] * dot(values, carried_out, 1, 1)
        gacts[1, :, lanes] = (gacts[1, :, lanes] + back) * slope
        back = mask_tail[...] * dot(keys, carried_out)
        gacts[2, :, lanes] = gacts[2, :, lanes] + back
        return 0

    lax.fori_loop(0, HEADS, backward_state, 0, unroll=True)
    grim_copy = links.start(gacts.at[:, pl.ds(0, 8)], grim, token_prev)
    ring_y.relay(2)
    rings_z[3].relay(4)

    def unconvolve(number, _):
        lanes = lanes_of(number)
        for stream in range(3):
            grad = gacts[stream, :, lanes]
            raw = proj[stream, :, lanes].astype(F32)
            both = jnp.concatenate([rim[stream, :, lanes].astype(F32), raw], axis=0)
            acc = taps[stream, 0:1, lanes] * grad
            row = 4 * stream
            tap_part[row : row + 1, lanes] = jnp.sum(grad * raw, axis=0, keepdims=True)
            for j in range(1, KW):
                acc = acc + taps[stream, j : j + 1, lanes] * (
                    pltpu.roll(grad, ROWS - j, 0) * mask_next[j - 1]
                )
                lagged = pltpu.roll(both, j, 0)[EDGE:]
                tap_part[row + j : row + j + 1, lanes] = jnp.sum(
                    grad * mask_back[j - 1] * lagged, axis=0, keepdims=True
                )
            gproj_out[stream, :, lanes] = acc.astype(BF)
        return 0

    tap_part[12:16, :] = jnp.zeros((4, WIDTH), F32)
    lax.fori_loop(0, 2, unconvolve, 0, unroll=True)

    ring_x2 = Ring(links, NZ, z, at_z, lambda to: gx2.at[to], gx2_half, gx2_block)
    ring_z2 = Ring(links, NX, x, at_x, lambda to: gz2.at[to], gz2_half, gz2_block)
    own, first, last = ring_x.finish()
    for k in range(NZ):
        value = own[k].astype(F32) + first[k].astype(F32) + last[k].astype(F32)
        gx2[k] = value.astype(BF).reshape(2, XROWS // 2, DH)
    ring_x2.begin()
    lax.fori_loop(2, HEADS, unconvolve, 0, unroll=True)
    tap_send[...] = tap_part[...].astype(BF)
    tap_copies = [
        links.start(tap_send, tap_in.at[z], at_z(wrap(z + k, NZ))) for k in range(1, NZ)
    ]
    tap_in[z] = tap_send[...]

    ring_x2.relay(2)
    for ring, band in zip(rings_z, order):
        own, first, last = ring.finish()
        for r in range(2):
            value = own[r].astype(F32) + first[r].astype(F32) + last[r].astype(F32)
            gz2[band, r] = value.astype(BF)
    ring_z2.begin()

    grim_copy.wait_recv()

    def unconvolve_rim(number, _):
        lanes = lanes_of(number)
        for stream in range(3):
            grad = gacts[stream, ROWS - EDGE : ROWS, lanes]
            both = jnp.concatenate([grad, grim[stream, :, lanes]], axis=0)
            acc = taps[stream, 0:1, lanes] * grad
            for j in range(1, KW):
                acc = acc + taps[stream, j : j + 1, lanes] * (
                    pltpu.roll(both, EDGE + 8 - j, 0)[0:EDGE]
                    * mask_next[j - 1, ROWS - EDGE : ROWS]
                )
            gproj_out[stream, ROWS - EDGE : ROWS, lanes] = acc.astype(BF)
        return 0

    ring_x2.relay(3)
    lax.fori_loop(0, HEADS, unconvolve_rim, 0, unroll=True)

    ring_z2.relay(2)

    for copy in tap_copies:
        copy.wait_recv()
    summed = tap_in[0].astype(F32)
    for k in range(1, NZ):
        summed = summed + tap_in[k].astype(F32)
    tap_row[...] = summed
    row_copies = [
        links.start(tap_row, tap_rowin.at[x], at_x(wrap(x + k, NX))) for k in range(1, NX)
    ]
    tap_rowin[x] = tap_row[...]

    own, first, last = ring_y.finish()
    for r in range(2):
        value = own[r].astype(F32) + first[r].astype(F32) + last[r].astype(F32)
        mixed_out[r * half : (r + 1) * half, :] = value.astype(BF)
    ring_x2.relay(4)

    for copy in row_copies:
        copy.wait_recv()
    summed = tap_rowin[0]
    for k in range(1, NX):
        summed = summed + tap_rowin[k]
    for stream in range(3):
        gtaps_out[stream] = summed[4 * stream : 4 * stream + 4, :]

    for ring, base, count in ((ring_z2, XROWS, ZROWS // 2), (ring_x2, 0, XROWS // 2)):
        own, first, last = ring.finish()
        for r in range(2):
            value = own[r].astype(F32) + first[r].astype(F32) + last[r].astype(F32)
            gweight_out[base + r * count : base + (r + 1) * count, :] = value
    links.drain()


def hand_over(*refs):
    sources, targets, sems = refs[:4], refs[4:8], refs[8]
    copies = [
        pltpu.make_async_copy(source, target, sems.at[k])
        for k, (source, target) in enumerate(zip(sources, targets))
    ]
    for copy in copies:
        copy.start()
    for copy in copies:
        copy.wait()


def body(projected, conv_weight, out_weight, out_grad, doc_lengths):
    vm = lambda *shape: pltpu.VMEM(shape, BF)
    vf = lambda *shape: pltpu.VMEM(shape, F32)
    piece = (DH // 2, DH)
    hops = lambda n, m, *tile: [vm(2, m // 2, *tile), vm(2, n // 2 - 1, m, *tile)]
    carry = [vm(NZ, *piece), vm(NZ, *piece), vm(*piece), vm(*piece), vm(NZ, *piece), vm(NZ, *piece)]
    scratch = [
        vm(3, ROWS, WIDTH), vm(WIDTH, 8 * WIDTH), vm(8, ROWS, WIDTH), vm(3, EDGE, WIDTH), vf(3, 8, WIDTH),
        vf(3, ROWS, DH), vf(3, ROWS, DH), vf(ROWS, DH), vf(ROWS, DH), vf(ROWS, ROWS),
        vm(ROWS, WIDTH), vm(ROWS, WIDTH), vm(ROWS, WIDTH), vm(HEADS, ROWS, ROWS), vf(ROWS, WIDTH),
        vf(HEADS, ROWS, DH), vf(ROWS, WIDTH), vm(ROWS, WIDTH), vm(WIDTH, ROWS), vm(ROWS, WIDTH),
        vm(ROWS, ROWS), vf(3, ROWS, WIDTH),
        *carry, *carry,
        vm(4, 2, 256, WIDTH), vm(4, 2, 256, WIDTH), vm(4, 2, 256, WIDTH), *hops(NY, 2, 256, WIDTH),
        vm(32, XROWS, DH), *hops(NX, NZ, XROWS, DH),
        vm(NZ, 2, XROWS // 2, DH), *hops(NZ, 2, XROWS // 2, DH),
        vm(NX, NZ, 2, ZROWS // 2, DH), vm(4, 2, 1, ZROWS // 2, DH), vm(4, 2, 3, 2, ZROWS // 2, DH),
        vm(NX, 2, ZROWS // 2, DH), *hops(NX, 2, ZROWS // 2, DH),
        vf(16, WIDTH), vm(16, WIDTH), vm(NZ, 16, WIDTH), vf(16, WIDTH), vf(NX, 16, WIDTH),
        pltpu.SemaphoreType.DMA((3,)), pltpu.SemaphoreType.DMA((COPIES,)), pltpu.SemaphoreType.DMA((COPIES,)),
    ]
    vmem = pl.BlockSpec(memory_space=pltpu.VMEM)
    outside = pl.BlockSpec(memory_space=pl.ANY)
    shapes = (
        jax.ShapeDtypeStruct((ROWS, WIDTH), BF),
        jax.ShapeDtypeStruct((3, ROWS, WIDTH), BF),
        jax.ShapeDtypeStruct((3, KW, WIDTH), F32),
        jax.ShapeDtypeStruct((WIDTH, DH), F32),
    )
    results = pl.pallas_call(
        kernel,
        out_shape=[pltpu.VMEM(shape.shape, shape.dtype) for shape in shapes],
        in_specs=[pl.BlockSpec(memory_space=pltpu.SMEM), outside, vmem, outside, outside],
        out_specs=[vmem] * 4,
        scratch_shapes=scratch,
        compiler_params=pltpu.CompilerParams(
            collective_id=0, has_side_effects=True, vmem_limit_bytes=58 * 2**20
        ),
        cost_estimate=pl.CostEstimate(
            flops=8 * 10**9, bytes_accessed=10**7, transcendentals=10**6
        ),
    )(doc_lengths, projected, conv_weight, out_weight, out_grad)
    return pl.pallas_call(
        hand_over,
        out_shape=shapes,
        in_specs=[outside] * 4,
        out_specs=(outside,) * 4,
        scratch_shapes=[pltpu.SemaphoreType.DMA((4,))],
        compiler_params=pltpu.CompilerParams(vmem_limit_bytes=2**20),
        cost_estimate=pl.CostEstimate(flops=0, bytes_accessed=5 * 10**6, transcendentals=0),
    )(*results)


def solution(mesh):
    return jax.shard_map(
        body,
        mesh=mesh,
        in_specs=(
            P(None, "seq", "head"),
            P(None, None, "head"),
            P("head", None),
            P("seq", "head"),
            P(),
        ),
        out_specs=(
            P("seq", "head"),
            P(None, "seq", "head"),
            P(None, None, "head"),
            P("head", "seq"),
        ),
        check_vma=False,
    )
```

```python
import jax
import jax.numpy as jnp
from jax import lax
from jax.experimental import pallas as pl
from jax.experimental.pallas import tpu as pltpu
from jax.sharding import PartitionSpec as P

DH = 128
KW = 4
HEADS = 4
ROWS = 512
WIDTH = 512
DOCS = 8
TOKENS = 16384
NX, NZ, NY = 4, 8, 4
EDGE = 16
BF = jnp.bfloat16
F32 = jnp.float32
MESH = pl.DeviceIdType.MESH
COPIES = 144
ZROWS = 320
XROWS = WIDTH - ZROWS


def wrap(value, size):
    return lax.rem(value + size, size)


def lanes_of(head):
    return pl.ds(pl.multiple_of(head * DH, DH), DH)


def dot(a, b, left=1, right=0):
    return lax.dot_general(a, b, (((left,), (right,)), ((), ())), preferred_element_type=F32)


class Links:
    def __init__(self, send_sems, recv_sems):
        self.send_sems, self.recv_sems = send_sems, recv_sems
        self.used, self.pending = 0, []

    def start(self, source, target, device):
        copy = pltpu.make_async_remote_copy(
            src_ref=source,
            dst_ref=target,
            send_sem=self.send_sems.at[self.used],
            recv_sem=self.recv_sems.at[self.used],
            device_id=device,
            device_id_type=MESH,
        )
        self.used += 1
        copy.start()
        self.pending.append(copy)
        return copy

    def drain(self):
        for copy in self.pending:
            copy.wait_send()


def add_into(target, source):
    for tile in range(target.shape[0]):
        target[tile] = (target[tile].astype(F32) + source[tile].astype(F32)).astype(BF)


class Ring:
    def __init__(self, links, n, me, device_of, own, halves, blocks):
        self.links, self.n, self.me = links, n, me
        self.device_of, self.own = device_of, own
        self.halves, self.blocks = halves, blocks
        self.arrivals = {}

    def part(self, way, ref, near):
        half = ref.shape[0] // 2
        first = (way == 0) == near
        return ref.at[pl.ds(0 if first else half, half)]

    def begin(self):
        far = self.n // 2
        for way, sign in ((0, 1), (1, -1)):
            there = self.device_of(wrap(self.me + sign, self.n))
            block = self.own(wrap(self.me + far, self.n))
            self.arrivals[way, 1] = [
                self.links.start(self.part(way, block, True), self.halves.at[way], there)
            ]
        for way, sign in ((0, 1), (1, -1)):
            there = self.device_of(wrap(self.me + sign, self.n))
            block = self.own(wrap(self.me + sign * (far - 1), self.n))
            self.arrivals[way, 2] = [
                self.links.start(
                    self.part(way, block, False),
                    self.part(way, self.blocks.at[way, 0], False),
                    there,
                )
            ]

    def relay(self, step):
        far = self.n // 2
        for way, sign in ((0, 1), (1, -1)):
            there = self.device_of(wrap(self.me + sign, self.n))
            block = self.own(wrap(self.me + sign * (far - step + 1), self.n))
            for copy in self.arrivals[way, step - 1]:
                copy.wait_recv()
            if step == 2:
                mine = self.part(way, block, True)
                add_into(mine, self.halves.at[way])
                landing = self.part(way, self.blocks.at[way, 0], True)
                self.arrivals[way, 2].append(self.links.start(mine, landing, there))
            else:
                add_into(block, self.blocks.at[way, step - 3])
                landing = self.blocks.at[way, step - 2]
                self.arrivals[way, step] = [self.links.start(block, landing, there)]

    def finish(self):
        last = self.n // 2
        for way in (0, 1):
            for copy in self.arrivals[way, last]:
                copy.wait_recv()
        return self.own(self.me), self.blocks.at[0, last - 2], self.blocks.at[1, last - 2]


def kernel(
    docs, proj_hbm, taps, weight_hbm, grad_hbm,
    mixed_out, gproj_out, gtaps_out, gweight_out,
    proj, weight, og, rim, grim,
    mask_back, mask_next, mask_head, mask_tail, allowed,
    qf, kf, val, probs, unit, scale, gunit, normed, normed_t, go, gprobs, gacts,
    fwd_send, fwd_in, fwd_row, fwd_rowin, fwd_out, state,
    bwd_send, bwd_in, bwd_row, bwd_rowin, bwd_out, gstate,
    sib_send, sib_recv, mix, mix_half, mix_block,
    gx, gx_half, gx_block, gx2, gx2_half, gx2_block,
    gz, gz_half, gz_block, gz2, gz2_half, gz2_block,
    tap_part, tap_send, tap_in, tap_row, tap_rowin,
    local_sems, send_sems, recv_sems,
):
    seq, head = lax.axis_index("seq"), lax.axis_index("head")
    x, z = seq // NZ, lax.rem(seq, NZ)
    y, core = head // 2, lax.rem(head, 2)
    at_x = lambda to: (to * NZ + z, head)
    at_z = lambda to: (x * NZ + to, head)
    at_y = lambda to: (seq, to * 2 + core)
    sibling = (seq, y * 2 + (1 - core))
    token_next = (wrap(seq + 1, NX * NZ), head)
    token_prev = (wrap(seq - 1, NX * NZ), head)
    links = Links(send_sems, recv_sems)

    partners = [sibling, at_y(wrap(y + 1, NY)), at_y(wrap(y - 1, NY)), token_next, token_prev]
    partners += [at_x(wrap(x + k, NX)) for k in range(1, NX)]
    partners += [at_z(wrap(z + k, NZ)) for k in range(1, NZ)]
    barrier = pltpu.get_barrier_semaphore()
    for partner in partners:
        pl.semaphore_signal(barrier, inc=1, device_id=partner, device_id_type=MESH)
    load_proj = pltpu.make_async_copy(proj_hbm, proj, local_sems.at[0])
    load_grad = pltpu.make_async_copy(grad_hbm, og.at[head], local_sems.at[1])
    load_weight = pltpu.make_async_copy(weight_hbm, weight, local_sems.at[2])
    load_proj.start()
    load_grad.start()
    load_weight.start()
    pl.semaphore_wait(barrier, len(partners))

    half = ROWS // 2
    up, down, across = wrap(y + 1, NY), wrap(y - 1, NY), wrap(y + 2, NY)
    block_of = lambda to: to * 2 + core
    upper, lower = pl.ds(0, half), pl.ds(half, half)
    top = lambda to: og.at[block_of(to), upper]
    bottom = lambda to: og.at[block_of(to), lower]
    whole = lambda to: og.at[block_of(to)]
    up_top = links.start(grad_hbm.at[upper], top(y), at_y(up))
    down_bottom = links.start(grad_hbm.at[lower], bottom(y), at_y(down))
    rim_copy = links.start(proj_hbm.at[:, pl.ds(ROWS - EDGE, EDGE)], rim, token_next)
    up_bottom = links.start(grad_hbm.at[lower], bottom(y), at_y(up))
    down_top = links.start(grad_hbm.at[upper], top(y), at_y(down))
    sib_own = links.start(grad_hbm, whole(y), sibling)

    starts = []
    total = jnp.int32(0)
    for i in range(DOCS):
        starts.append(total)
        total = total + docs[i]
    offset = seq * ROWS

    def doc_at(position):
        count = jnp.int32(0)
        for start in starts:
            count = count + jnp.where(start <= position, 1, 0)
        return count

    ends = [doc_at((x * NZ + k) * ROWS - 1) for k in range(NZ + 1)]
    same = lambda a, b: jnp.where(ends[a] == ends[b], jnp.float32(1), jnp.float32(0))

    position = offset + lax.broadcasted_iota(jnp.int32, (ROWS, DH), 0)
    doc_start = jnp.zeros((ROWS, DH), jnp.int32)
    doc_end = jnp.full((ROWS, DH), TOKENS, jnp.int32)
    for i in range(1, DOCS):
        doc_start = jnp.where(starts[i] <= position, starts[i], doc_start)
    for i in range(DOCS - 1, 0, -1):
        doc_end = jnp.where(starts[i] > position, starts[i], doc_end)
    one, zero = jnp.float32(1), jnp.float32(0)
    for j in range(1, KW):
        mask_back[j - 1] = jnp.where(position - j >= doc_start, one, zero)
        mask_next[j - 1] = jnp.where(position + j < doc_end, one, zero)
    mask_head[...] = jnp.where(doc_start < offset, one, zero)
    mask_tail[...] = jnp.where(doc_end > offset + ROWS - 1, one, zero)
    for tile in range(ROWS // DH):
        column = offset + tile * DH + lax.broadcasted_iota(jnp.int32, (ROWS, DH), 1)
        allowed[:, tile * DH : (tile + 1) * DH] = jnp.where(
            (column <= position) & (column >= doc_start), one, zero
        )

    load_proj.wait()

    def activate(stream, acc, rows, lanes):
        act = acc.astype(BF)
        if stream == 2:
            val[rows, lanes] = act
        else:
            wide = act.astype(F32)
            feature = jnp.where(wide > 0, wide + 1.0, jnp.exp(jnp.minimum(wide, 0.0)))
            (qf, kf)[stream][rows, lanes] = feature.astype(BF)

    def convolve(number, _):
        lanes = lanes_of(number)
        for stream in range(3):
            raw = proj[stream, :, lanes].astype(F32)
            acc = taps[stream, 0:1, lanes] * raw
            for j in range(1, KW):
                acc = acc + taps[stream, j : j + 1, lanes] * (
                    pltpu.roll(raw, j, 0) * mask_back[j - 1]
                )
            activate(stream, acc, slice(None), lanes)
        return 0

    lax.fori_loop(0, HEADS, convolve, 0, unroll=True)
    rim_copy.wait_recv()

    def convolve_rim(number, _):
        lanes = lanes_of(number)
        for stream in range(3):
            raw = proj[stream, 0:EDGE, lanes].astype(F32)
            both = jnp.concatenate([rim[stream, :, lanes].astype(F32), raw], axis=0)
            acc = taps[stream, 0:1, lanes] * raw
            for j in range(1, KW):
                acc = acc + taps[stream, j : j + 1, lanes] * (
                    pltpu.roll(both, j, 0)[EDGE:] * mask_back[j - 1, 0:EDGE]
                )
            activate(stream, acc, slice(0, EDGE), lanes)
        return 0

    lax.fori_loop(0, HEADS, convolve_rim, 0, unroll=True)

    def tail_state(number, _):
        lanes = lanes_of(number)
        keys = (kf[:, lanes].astype(F32) * mask_tail[...]).astype(BF)
        local = dot(keys, val[:, lanes], 0, 0)
        fwd_send[pl.ds(2 * number, 2)] = local.astype(BF).reshape(2, DH // 2, DH)
        return 0

    def to_owners(send, landing):
        return [
            links.start(send.at[wrap(z + k, NZ)], landing.at[z], at_z(wrap(z + k, NZ)))
            for k in range(1, NZ)
        ]

    lax.fori_loop(0, HEADS, tail_state, 0, unroll=True)
    fwd_copies = to_owners(fwd_send, fwd_in)
    fwd_in[z] = fwd_send[z]

    up_top.wait_recv()
    pass_top = links.start(top(down), top(down), at_y(up))
    down_bottom.wait_recv()
    pass_bottom = links.start(bottom(up), bottom(up), at_y(down))

    def local_attention(number, _):
        lanes = lanes_of(number)
        for r in range(ROWS // DH):
            rows, width = slice(r * DH, (r + 1) * DH), (r + 1) * DH
            scores = dot(qf[rows, lanes], kf[0:width, lanes], 1, 1)
            kept = (scores * allowed[rows, 0:width]).astype(BF)
            probs[number, rows, 0:width] = kept
            unit[rows, lanes] = dot(kept, val[0:width, lanes])
        return 0

    lax.fori_loop(0, HEADS, local_attention, 0, unroll=True)

    for copy in fwd_copies:
        copy.wait_recv()
    run = jnp.zeros((DH // 2, DH), F32)
    prefix = []
    for k in range(NZ):
        prefix.append(run)
        run = fwd_in[k].astype(F32) + same(k, k + 1) * run
    fwd_row[...] = run.astype(BF)
    row_copy = links.start(fwd_row, fwd_rowin, at_x(wrap(x + 1, NX)))

    load_grad.wait()
    load_weight.wait()

    def add_gunit(block, first=False):
        columns = pl.ds(pl.multiple_of(block * WIDTH, WIDTH), WIDTH)

        def tile(r, _):
            rows = pl.ds(pl.multiple_of(r * 256, 256), 256)
            part = dot(og[block, rows, :], weight[:, columns], 1, 1)
            gunit[rows, :] = part if first else gunit[rows, :] + part
            return 0

        lax.fori_loop(0, ROWS // 256, tile, 0, unroll=True)

    add_gunit(block_of(y), True)
    row_copy.wait_recv()
    carried = fwd_rowin[...].astype(F32)
    for k in range(NZ):
        fwd_out[k] = (prefix[k] + same(k, 0) * carried).astype(BF)
    out_copies = to_owners(fwd_out, state)
    state[z] = fwd_out[z]

    other = lambda to: to * 2 + (1 - core)
    sib_own.wait_recv()
    add_gunit(other(y))
    up_bottom.wait_recv()
    sib_down = links.start(whole(down), whole(down), sibling)
    down_top.wait_recv()
    sib_up = links.start(whole(up), whole(up), sibling)

    for copy in out_copies:
        copy.wait_recv()

    def finish_attention(number, _):
        lanes = lanes_of(number)
        carried_in = state[pl.ds(2 * number, 2)].reshape(DH, DH)
        attn = unit[:, lanes] + mask_head[...] * dot(qf[:, lanes], carried_in)
        factor = lax.rsqrt(jnp.mean(attn * attn, axis=1, keepdims=True) + 1e-06)
        scaled = attn * factor
        unit[:, lanes] = scaled
        scale[number] = jnp.broadcast_to(factor, (ROWS, DH))
        normed[:, lanes] = scaled.astype(BF)
        normed_t[lanes_of(number), :] = scaled.T.astype(BF)
        return 0

    lax.fori_loop(0, HEADS, finish_attention, 0, unroll=True)

    def weight_band(band):
        def one_block(which, _):
            block = band * 2 + which
            part = dot(normed_t[0:XROWS, :], og[block]).astype(BF)
            for j in range(4):
                gx[block * 4 + j] = part[:, j * DH : (j + 1) * DH]
            part = dot(normed_t[XROWS:WIDTH, :], og[block]).astype(BF)
            for j in range(4):
                tile = part[:, j * DH : (j + 1) * DH]
                gz[band, which * 4 + j] = tile.reshape(2, ZROWS // 2, DH)
            return 0

        lax.fori_loop(0, 2, one_block, 0, unroll=True)

    ring_x = Ring(links, NX, x, at_x, lambda to: gx.at[pl.ds(to * NZ, NZ)], gx_half, gx_block)
    order = [y, down, up, across]
    rings_z = [
        Ring(links, NZ, z, at_z, lambda to, b=b: gz.at[b, to], gz_half.at[k], gz_block.at[k])
        for k, b in enumerate(order)
    ]
    weight_band(y)
    rings_z[0].begin()
    add_gunit(block_of(down))
    add_gunit(block_of(up))
    sib_down.wait_recv()
    weight_band(down)
    rings_z[1].begin()
    pass_top.wait_recv()
    pass_bottom.wait_recv()
    sib_across = links.start(whole(across), whole(across), sibling)
    sib_up.wait_recv()
    weight_band(up)
    rings_z[2].begin()
    add_gunit(other(down))
    add_gunit(other(up))
    add_gunit(block_of(across))
    sib_across.wait_recv()
    add_gunit(other(across))
    weight_band(across)
    ring_x.begin()
    rings_z[3].begin()

    def grad_attn(number, _):
        lanes = lanes_of(number)
        given, scaled = gunit[:, lanes], unit[:, lanes]
        inner = jnp.mean(given * scaled, axis=1, keepdims=True)
        grad = (scale[number] * (given - scaled * inner)).astype(BF)
        go[:, lanes] = grad
        queries = (qf[:, lanes].astype(F32) * mask_head[...]).astype(BF)
        local = dot(queries, grad, 0, 0)
        bwd_send[pl.ds(2 * number, 2)] = local.astype(BF).reshape(2, DH // 2, DH)
        return 0

    lax.fori_loop(0, HEADS, grad_attn, 0, unroll=True)
    bwd_copies = to_owners(bwd_send, bwd_in)
    bwd_in[z] = bwd_send[z]
    rings_z[0].relay(2)

    ring_y = Ring(links, NY, y, at_y, lambda to: mix.at[to], mix_half, mix_block)
    outward = [across, up, down]

    def project(block, put):
        columns = pl.ds(pl.multiple_of(block * WIDTH, WIDTH), WIDTH)

        def tile(r, _):
            rows = pl.ds(pl.multiple_of(r * half, half), half)
            put(r, dot(normed[rows, :], weight[:, columns]))
            return 0

        lax.fori_loop(0, 2, tile, 0, unroll=True)

    sib_copies = []
    for k, to in enumerate(outward + [y]):

        def put_sib(r, part, k=k):
            sib_send[k, r] = part.astype(BF)

        project(other(to), put_sib)
        sib_copies.append(links.start(sib_send.at[k], sib_recv.at[k], sibling))

    def put_own(k, to):
        sib_copies[k].wait_recv()

        def put(r, part):
            mix[to, r] = (part + sib_recv[k, r].astype(F32)).astype(BF)

        project(block_of(to), put)

    rings_z[1].relay(2)
    rings_z[2].relay(2)
    rings_z[0].relay(3)

    for copy in bwd_copies:
        copy.wait_recv()
    run = jnp.zeros((DH // 2, DH), F32)
    suffix = [None] * NZ
    for k in range(NZ - 1, -1, -1):
        suffix[k] = run
        run = bwd_in[k].astype(F32) + same(k, k + 1) * run
    bwd_row[...] = run.astype(BF)
    back_copy = links.start(bwd_row, bwd_rowin, at_x(wrap(x - 1, NX)))

    for k, to in enumerate(outward):
        put_own(k, to)
    ring_y.begin()
    rings_z[3].relay(2)
    rings_z[1].relay(3)
    rings_z[2].relay(3)
    rings_z[0].relay(4)
    ring_x.relay(2)

    def backward_local(number, _):
        lanes = lanes_of(number)
        for r in range(ROWS // DH):
            rows, width = slice(r * DH, (r + 1) * DH), (r + 1) * DH
            scores = dot(go[rows, lanes], val[0:width, lanes], 1, 1)
            kept = (scores * allowed[rows, 0:width]).astype(BF)
            gprobs[rows, 0:width] = kept
            gacts[0, rows, lanes] = dot(kept, kf[0:width, lanes])
        for r in range(ROWS // DH):
            rows, below = slice(r * DH, (r + 1) * DH), slice(r * DH, ROWS)
            gacts[1, rows, lanes] = dot(gprobs[below, rows], qf[below, lanes], 0, 0)
            gacts[2, rows, lanes] = dot(probs[number, below, rows], go[below, lanes], 0, 0)
        return 0

    back_copy.wait_recv()
    carried = bwd_rowin[...].astype(F32)
    for k in range(NZ):
        bwd_out[k] = (suffix[k] + same(k + 1, NZ) * carried).astype(BF)
    gout_copies = to_owners(bwd_out, gstate)
    gstate[z] = bwd_out[z]

    lax.fori_loop(0, HEADS, backward_local, 0, unroll=True)
    rings_z[3].relay(3)
    rings_z[1].relay(4)
    rings_z[2].relay(4)
    put_own(3, y)

    for copy in gout_copies:
        copy.wait_recv()

    def backward_state(number, _):
        lanes = lanes_of(number)
        carried_in = state[pl.ds(2 * number, 2)].reshape(DH, DH)
        carried_out = gstate[pl.ds(2 * number, 2)].reshape(DH, DH)
        queries, keys, values = qf[:, lanes], kf[:, lanes], val[:, lanes]
        slope = jnp.minimum(queries.astype(F32), 1.0)
        back = mask_head[...] * dot(go[:, lanes], carried_in, 1, 1)
        gacts[0, :, lanes] = (gacts[0, :, lanes] + back) * slope
        slope = jnp.minimum(keys.astype(F32), 1.0)
        back = mask_tail[...] * dot(values, carried_out, 1, 1)
        gacts[1, :, lanes] = (gacts[1, :, lanes] + back) * slope
        back = mask_tail[...] * dot(keys, carried_out)
        gacts[2, :, lanes] = gacts[2, :, lanes] + back
        return 0

    lax.fori_loop(0, HEADS, backward_state, 0, unroll=True)
    grim_copy = links.start(gacts.at[:, pl.ds(0, 8)], grim, token_prev)
    ring_y.relay(2)
    rings_z[3].relay(4)

    def unconvolve(number, _):
        lanes = lanes_of(number)
        for stream in range(3):
            grad = gacts[stream, :, lanes]
            raw = proj[stream, :, lanes].astype(F32)
            both = jnp.concatenate([rim[stream, :, lanes].astype(F32), raw], axis=0)
            acc = taps[stream, 0:1, lanes] * grad
            row = 4 * stream
            tap_part[row : row + 1, lanes] = jnp.sum(grad * raw, axis=0, keepdims=True)
            for j in range(1, KW):
                acc = acc + taps[stream, j : j + 1, lanes] * (
                    pltpu.roll(grad, ROWS - j, 0) * mask_next[j - 1]
                )
                lagged = pltpu.roll(both, j, 0)[EDGE:]
                tap_part[row + j : row + j + 1, lanes] = jnp.sum(
                    grad * mask_back[j - 1] * lagged, axis=0, keepdims=True
                )
            gproj_out[stream, :, lanes] = acc.astype(BF)
        return 0

    tap_part[12:16, :] = jnp.zeros((4, WIDTH), F32)
    lax.fori_loop(0, 2, unconvolve, 0, unroll=True)

    ring_x2 = Ring(links, NZ, z, at_z, lambda to: gx2.at[to], gx2_half, gx2_block)
    ring_z2 = Ring(links, NX, x, at_x, lambda to: gz2.at[to], gz2_half, gz2_block)
    own, first, last = ring_x.finish()
    for k in range(NZ):
        value = own[k].astype(F32) + first[k].astype(F32) + last[k].astype(F32)
        gx2[k] = value.astype(BF).reshape(2, XROWS // 2, DH)
    ring_x2.begin()
    lax.fori_loop(2, HEADS, unconvolve, 0, unroll=True)
    tap_send[...] = tap_part[...].astype(BF)
    tap_copies = [
        links.start(tap_send, tap_in.at[z], at_z(wrap(z + k, NZ))) for k in range(1, NZ)
    ]
    tap_in[z] = tap_send[...]

    ring_x2.relay(2)
    for ring, band in zip(rings_z, order):
        own, first, last = ring.finish()
        for r in range(2):
            value = own[r].astype(F32) + first[r].astype(F32) + last[r].astype(F32)
            gz2[band, r] = value.astype(BF)
    ring_z2.begin()

    grim_copy.wait_recv()

    def unconvolve_rim(number, _):
        lanes = lanes_of(number)
        for stream in range(3):
            grad = gacts[stream, ROWS - EDGE : ROWS, lanes]
            both = jnp.concatenate([grad, grim[stream, :, lanes]], axis=0)
            acc = taps[stream, 0:1, lanes] * grad
            for j in range(1, KW):
                acc = acc + taps[stream, j : j + 1, lanes] * (
                    pltpu.roll(both, EDGE + 8 - j, 0)[0:EDGE]
                    * mask_next[j - 1, ROWS - EDGE : ROWS]
                )
            gproj_out[stream, ROWS - EDGE : ROWS, lanes] = acc.astype(BF)
        return 0

    ring_x2.relay(3)
    lax.fori_loop(0, HEADS, unconvolve_rim, 0, unroll=True)

    ring_z2.relay(2)

    for copy in tap_copies:
        copy.wait_recv()
    summed = tap_in[0].astype(F32)
    for k in range(1, NZ):
        summed = summed + tap_in[k].astype(F32)
    tap_row[...] = summed
    row_copies = [
        links.start(tap_row, tap_rowin.at[x], at_x(wrap(x + k, NX))) for k in range(1, NX)
    ]
    tap_rowin[x] = tap_row[...]

    own, first, last = ring_y.finish()
    for r in range(2):
        value = own[r].astype(F32) + first[r].astype(F32) + last[r].astype(F32)
        mixed_out[r * half : (r + 1) * half, :] = value.astype(BF)
    ring_x2.relay(4)

    for copy in row_copies:
        copy.wait_recv()
    summed = tap_rowin[0]
    for k in range(1, NX):
        summed = summed + tap_rowin[k]
    for stream in range(3):
        gtaps_out[stream] = summed[4 * stream : 4 * stream + 4, :]

    for ring, base, count in ((ring_z2, XROWS, ZROWS // 2), (ring_x2, 0, XROWS // 2)):
        own, first, last = ring.finish()
        for r in range(2):
            value = own[r].astype(F32) + first[r].astype(F32) + last[r].astype(F32)
            gweight_out[base + r * count : base + (r + 1) * count, :] = value
    links.drain()


def hand_over(*refs):
    sources, targets, sems = refs[:4], refs[4:8], refs[8]
    copies = [
        pltpu.make_async_copy(source, target, sems.at[k])
        for k, (source, target) in enumerate(zip(sources, targets))
    ]
    for copy in copies:
        copy.start()
    for copy in copies:
        copy.wait()


def body(projected, conv_weight, out_weight, out_grad, doc_lengths):
    vm = lambda *shape: pltpu.VMEM(shape, BF)
    vf = lambda *shape: pltpu.VMEM(shape, F32)
    piece = (DH // 2, DH)
    hops = lambda n, m, *tile: [vm(2, m // 2, *tile), vm(2, n // 2 - 1, m, *tile)]
    carry = [vm(NZ, *piece), vm(NZ, *piece), vm(*piece), vm(*piece), vm(NZ, *piece), vm(NZ, *piece)]
    scratch = [
        vm(3, ROWS, WIDTH), vm(WIDTH, 8 * WIDTH), vm(8, ROWS, WIDTH), vm(3, EDGE, WIDTH), vf(3, 8, WIDTH),
        vf(3, ROWS, DH), vf(3, ROWS, DH), vf(ROWS, DH), vf(ROWS, DH), vf(ROWS, ROWS),
        vm(ROWS, WIDTH), vm(ROWS, WIDTH), vm(ROWS, WIDTH), vm(HEADS, ROWS, ROWS), vf(ROWS, WIDTH),
        vf(HEADS, ROWS, DH), vf(ROWS, WIDTH), vm(ROWS, WIDTH), vm(WIDTH, ROWS), vm(ROWS, WIDTH),
        vm(ROWS, ROWS), vf(3, ROWS, WIDTH),
        *carry, *carry,
        vm(4, 2, 256, WIDTH), vm(4, 2, 256, WIDTH), vm(4, 2, 256, WIDTH), *hops(NY, 2, 256, WIDTH),
        vm(32, XROWS, DH), *hops(NX, NZ, XROWS, DH),
        vm(NZ, 2, XROWS // 2, DH), *hops(NZ, 2, XROWS // 2, DH),
        vm(NX, NZ, 2, ZROWS // 2, DH), vm(4, 2, 1, ZROWS // 2, DH), vm(4, 2, 3, 2, ZROWS // 2, DH),
        vm(NX, 2, ZROWS // 2, DH), *hops(NX, 2, ZROWS // 2, DH),
        vf(16, WIDTH), vm(16, WIDTH), vm(NZ, 16, WIDTH), vf(16, WIDTH), vf(NX, 16, WIDTH),
        pltpu.SemaphoreType.DMA((3,)), pltpu.SemaphoreType.DMA((COPIES,)), pltpu.SemaphoreType.DMA((COPIES,)),
    ]
    vmem = pl.BlockSpec(memory_space=pltpu.VMEM)
    outside = pl.BlockSpec(memory_space=pl.ANY)
    shapes = (
        jax.ShapeDtypeStruct((ROWS, WIDTH), BF),
        jax.ShapeDtypeStruct((3, ROWS, WIDTH), BF),
        jax.ShapeDtypeStruct((3, KW, WIDTH), F32),
        jax.ShapeDtypeStruct((WIDTH, DH), F32),
    )
    results = pl.pallas_call(
        kernel,
        out_shape=[pltpu.VMEM(shape.shape, shape.dtype) for shape in shapes],
        in_specs=[pl.BlockSpec(memory_space=pltpu.SMEM), outside, vmem, outside, outside],
        out_specs=[vmem] * 4,
        scratch_shapes=scratch,
        compiler_params=pltpu.CompilerParams(
            collective_id=0, has_side_effects=True, vmem_limit_bytes=58 * 2**20
        ),
        cost_estimate=pl.CostEstimate(
            flops=8 * 10**9, bytes_accessed=10**7, transcendentals=10**6
        ),
    )(doc_lengths, projected, conv_weight, out_weight, out_grad)
    return pl.pallas_call(
        hand_over,
        out_shape=shapes,
        in_specs=[outside] * 4,
        out_specs=(outside,) * 4,
        scratch_shapes=[pltpu.SemaphoreType.DMA((4,))],
        compiler_params=pltpu.CompilerParams(vmem_limit_bytes=2**20),
        cost_estimate=pl.CostEstimate(flops=0, bytes_accessed=5 * 10**6, transcendentals=0),
    )(*results)


def solution(mesh):
    return jax.shard_map(
        body,
        mesh=mesh,
        in_specs=(
            P(None, "seq", "head"),
            P(None, None, "head"),
            P("head", None),
            P("seq", "head"),
            P(),
        ),
        out_specs=(
            P("seq", "head"),
            P(None, "seq", "head"),
            P(None, None, "head"),
            P("head", "seq"),
        ),
        check_vma=False,
    )
```

```python
import jax
import jax.numpy as jnp
from jax import lax
from jax.experimental import pallas as pl
from jax.experimental.pallas import tpu as pltpu
from jax.sharding import PartitionSpec as P

DH = 128
KW = 4
HEADS = 4
ROWS = 512
WIDTH = 512
DOCS = 8
TOKENS = 16384
NX, NZ, NY = 4, 8, 4
EDGE = 16
BF = jnp.bfloat16
F32 = jnp.float32
MESH = pl.DeviceIdType.MESH
COPIES = 144
ZROWS = 256
XROWS = WIDTH - ZROWS


def wrap(value, size):
    return lax.rem(value + size, size)


def lanes_of(head):
    return pl.ds(pl.multiple_of(head * DH, DH), DH)


def dot(a, b, left=1, right=0):
    return lax.dot_general(a, b, (((left,), (right,)), ((), ())), preferred_element_type=F32)


class Links:
    def __init__(self, send_sems, recv_sems):
        self.send_sems, self.recv_sems = send_sems, recv_sems
        self.used, self.pending = 0, []

    def start(self, source, target, device):
        copy = pltpu.make_async_remote_copy(
            src_ref=source,
            dst_ref=target,
            send_sem=self.send_sems.at[self.used],
            recv_sem=self.recv_sems.at[self.used],
            device_id=device,
            device_id_type=MESH,
        )
        self.used += 1
        copy.start()
        self.pending.append(copy)
        return copy

    def drain(self):
        for copy in self.pending:
            copy.wait_send()


def add_into(target, source):
    for tile in range(target.shape[0]):
        target[tile] = (target[tile].astype(F32) + source[tile].astype(F32)).astype(BF)


class Ring:
    def __init__(self, links, n, me, device_of, own, halves, blocks):
        self.links, self.n, self.me = links, n, me
        self.device_of, self.own = device_of, own
        self.halves, self.blocks = halves, blocks
        self.arrivals = {}

    def part(self, way, ref, near):
        half = ref.shape[0] // 2
        first = (way == 0) == near
        return ref.at[pl.ds(0 if first else half, half)]

    def begin(self):
        far = self.n // 2
        for way, sign in ((0, 1), (1, -1)):
            there = self.device_of(wrap(self.me + sign, self.n))
            block = self.own(wrap(self.me + far, self.n))
            self.arrivals[way, 1] = [
                self.links.start(self.part(way, block, True), self.halves.at[way], there)
            ]
        for way, sign in ((0, 1), (1, -1)):
            there = self.device_of(wrap(self.me + sign, self.n))
            block = self.own(wrap(self.me + sign * (far - 1), self.n))
            self.arrivals[way, 2] = [
                self.links.start(
                    self.part(way, block, False),
                    self.part(way, self.blocks.at[way, 0], False),
                    there,
                )
            ]

    def relay(self, step):
        far = self.n // 2
        for way, sign in ((0, 1), (1, -1)):
            there = self.device_of(wrap(self.me + sign, self.n))
            block = self.own(wrap(self.me + sign * (far - step + 1), self.n))
            for copy in self.arrivals[way, step - 1]:
                copy.wait_recv()
            if step == 2:
                mine = self.part(way, block, True)
                add_into(mine, self.halves.at[way])
                landing = self.part(way, self.blocks.at[way, 0], True)
                self.arrivals[way, 2].append(self.links.start(mine, landing, there))
            else:
                add_into(block, self.blocks.at[way, step - 3])
                landing = self.blocks.at[way, step - 2]
                self.arrivals[way, step] = [self.links.start(block, landing, there)]

    def finish(self):
        last = self.n // 2
        for way in (0, 1):
            for copy in self.arrivals[way, last]:
                copy.wait_recv()
        return self.own(self.me), self.blocks.at[0, last - 2], self.blocks.at[1, last - 2]


def kernel(
    docs, proj_hbm, taps, weight_hbm, grad_hbm,
    mixed_out, gproj_out, gtaps_out, gweight_out,
    proj, weight, og, rim, grim,
    mask_back, mask_next, mask_head, mask_tail, allowed,
    qf, kf, val, probs, unit, scale, gunit, normed, normed_t, go, gprobs, gacts,
    fwd_send, fwd_in, fwd_row, fwd_rowin, fwd_out, state,
    bwd_send, bwd_in, bwd_row, bwd_rowin, bwd_out, gstate,
    sib_send, sib_recv, mix, mix_half, mix_block,
    gx, gx_half, gx_block, gx2, gx2_half, gx2_block,
    gz, gz_half, gz_block, gz2, gz2_half, gz2_block,
    tap_part, tap_send, tap_in, tap_row, tap_rowin,
    local_sems, send_sems, recv_sems,
):
    seq, head = lax.axis_index("seq"), lax.axis_index("head")
    x, z = seq // NZ, lax.rem(seq, NZ)
    y, core = head // 2, lax.rem(head, 2)
    at_x = lambda to: (to * NZ + z, head)
    at_z = lambda to: (x * NZ + to, head)
    at_y = lambda to: (seq, to * 2 + core)
    sibling = (seq, y * 2 + (1 - core))
    token_next = (wrap(seq + 1, NX * NZ), head)
    token_prev = (wrap(seq - 1, NX * NZ), head)
    links = Links(send_sems, recv_sems)

    partners = [sibling, at_y(wrap(y + 1, NY)), at_y(wrap(y - 1, NY)), token_next, token_prev]
    partners += [at_x(wrap(x + k, NX)) for k in range(1, NX)]
    partners += [at_z(wrap(z + k, NZ)) for k in range(1, NZ)]
    barrier = pltpu.get_barrier_semaphore()
    for partner in partners:
        pl.semaphore_signal(barrier, inc=1, device_id=partner, device_id_type=MESH)
    load_proj = pltpu.make_async_copy(proj_hbm, proj, local_sems.at[0])
    load_grad = pltpu.make_async_copy(grad_hbm, og.at[head], local_sems.at[1])
    load_weight = pltpu.make_async_copy(weight_hbm, weight, local_sems.at[2])
    load_proj.start()
    load_grad.start()
    load_weight.start()
    pl.semaphore_wait(barrier, len(partners))

    half = ROWS // 2
    up, down, across = wrap(y + 1, NY), wrap(y - 1, NY), wrap(y + 2, NY)
    block_of = lambda to: to * 2 + core
    upper, lower = pl.ds(0, half), pl.ds(half, half)
    top = lambda to: og.at[block_of(to), upper]
    bottom = lambda to: og.at[block_of(to), lower]
    whole = lambda to: og.at[block_of(to)]
    up_top = links.start(grad_hbm.at[upper], top(y), at_y(up))
    down_bottom = links.start(grad_hbm.at[lower], bottom(y), at_y(down))
    rim_copy = links.start(proj_hbm.at[:, pl.ds(ROWS - EDGE, EDGE)], rim, token_next)
    up_bottom = links.start(grad_hbm.at[lower], bottom(y), at_y(up))
    down_top = links.start(grad_hbm.at[upper], top(y), at_y(down))
    sib_own = links.start(grad_hbm, whole(y), sibling)

    starts = []
    total = jnp.int32(0)
    for i in range(DOCS):
        starts.append(total)
        total = total + docs[i]
    offset = seq * ROWS

    def doc_at(position):
        count = jnp.int32(0)
        for start in starts:
            count = count + jnp.where(start <= position, 1, 0)
        return count

    ends = [doc_at((x * NZ + k) * ROWS - 1) for k in range(NZ + 1)]
    same = lambda a, b: jnp.where(ends[a] == ends[b], jnp.float32(1), jnp.float32(0))

    position = offset + lax.broadcasted_iota(jnp.int32, (ROWS, DH), 0)
    doc_start = jnp.zeros((ROWS, DH), jnp.int32)
    doc_end = jnp.full((ROWS, DH), TOKENS, jnp.int32)
    for i in range(1, DOCS):
        doc_start = jnp.where(starts[i] <= position, starts[i], doc_start)
    for i in range(DOCS - 1, 0, -1):
        doc_end = jnp.where(starts[i] > position, starts[i], doc_end)
    one, zero = jnp.float32(1), jnp.float32(0)
    for j in range(1, KW):
        mask_back[j - 1] = jnp.where(position - j >= doc_start, one, zero)
        mask_next[j - 1] = jnp.where(position + j < doc_end, one, zero)
    mask_head[...] = jnp.where(doc_start < offset, one, zero)
    mask_tail[...] = jnp.where(doc_end > offset + ROWS - 1, one, zero)
    for tile in range(ROWS // DH):
        column = offset + tile * DH + lax.broadcasted_iota(jnp.int32, (ROWS, DH), 1)
        allowed[:, tile * DH : (tile + 1) * DH] = jnp.where(
            (column <= position) & (column >= doc_start), one, zero
        )

    load_proj.wait()

    def activate(stream, acc, rows, lanes):
        act = acc.astype(BF)
        if stream == 2:
            val[rows, lanes] = act
        else:
            wide = act.astype(F32)
            feature = jnp.where(wide > 0, wide + 1.0, jnp.exp(jnp.minimum(wide, 0.0)))
            (qf, kf)[stream][rows, lanes] = feature.astype(BF)

    def convolve(number, _):
        lanes = lanes_of(number)
        for stream in range(3):
            raw = proj[stream, :, lanes].astype(F32)
            acc = taps[stream, 0:1, lanes] * raw
            for j in range(1, KW):
                acc = acc + taps[stream, j : j + 1, lanes] * (
                    pltpu.roll(raw, j, 0) * mask_back[j - 1]
                )
            activate(stream, acc, slice(None), lanes)
        return 0

    lax.fori_loop(0, HEADS, convolve, 0, unroll=True)
    rim_copy.wait_recv()

    def convolve_rim(number, _):
        lanes = lanes_of(number)
        for stream in range(3):
            raw = proj[stream, 0:EDGE, lanes].astype(F32)
            both = jnp.concatenate([rim[stream, :, lanes].astype(F32), raw], axis=0)
            acc = taps[stream, 0:1, lanes] * raw
            for j in range(1, KW):
                acc = acc + taps[stream, j : j + 1, lanes] * (
                    pltpu.roll(both, j, 0)[EDGE:] * mask_back[j - 1, 0:EDGE]
                )
            activate(stream, acc, slice(0, EDGE), lanes)
        return 0

    lax.fori_loop(0, HEADS, convolve_rim, 0, unroll=True)

    def tail_state(number, _):
        lanes = lanes_of(number)
        keys = (kf[:, lanes].astype(F32) * mask_tail[...]).astype(BF)
        local = dot(keys, val[:, lanes], 0, 0)
        fwd_send[pl.ds(2 * number, 2)] = local.astype(BF).reshape(2, DH // 2, DH)
        return 0

    def to_owners(send, landing):
        return [
            links.start(send.at[wrap(z + k, NZ)], landing.at[z], at_z(wrap(z + k, NZ)))
            for k in range(1, NZ)
        ]

    lax.fori_loop(0, HEADS, tail_state, 0, unroll=True)
    fwd_copies = to_owners(fwd_send, fwd_in)
    fwd_in[z] = fwd_send[z]

    up_top.wait_recv()
    pass_top = links.start(top(down), top(down), at_y(up))
    down_bottom.wait_recv()
    pass_bottom = links.start(bottom(up), bottom(up), at_y(down))

    def local_attention(number, _):
        lanes = lanes_of(number)
        for r in range(ROWS // DH):
            rows, width = slice(r * DH, (r + 1) * DH), (r + 1) * DH
            scores = dot(qf[rows, lanes], kf[0:width, lanes], 1, 1)
            kept = (scores * allowed[rows, 0:width]).astype(BF)
            probs[number, rows, 0:width] = kept
            unit[rows, lanes] = dot(kept, val[0:width, lanes])
        return 0

    lax.fori_loop(0, HEADS, local_attention, 0, unroll=True)

    for copy in fwd_copies:
        copy.wait_recv()
    run = jnp.zeros((DH // 2, DH), F32)
    prefix = []
    for k in range(NZ):
        prefix.append(run)
        run = fwd_in[k].astype(F32) + same(k, k + 1) * run
    fwd_row[...] = run.astype(BF)
    row_copy = links.start(fwd_row, fwd_rowin, at_x(wrap(x + 1, NX)))

    load_grad.wait()
    load_weight.wait()

    def add_gunit(block, first=False):
        columns = pl.ds(pl.multiple_of(block * WIDTH, WIDTH), WIDTH)

        def tile(r, _):
            rows = pl.ds(pl.multiple_of(r * 256, 256), 256)
            part = dot(og[block, rows, :], weight[:, columns], 1, 1)
            gunit[rows, :] = part if first else gunit[rows, :] + part
            return 0

        lax.fori_loop(0, ROWS // 256, tile, 0, unroll=True)

    add_gunit(block_of(y), True)
    row_copy.wait_recv()
    carried = fwd_rowin[...].astype(F32)
    for k in range(NZ):
        fwd_out[k] = (prefix[k] + same(k, 0) * carried).astype(BF)
    out_copies = to_owners(fwd_out, state)
    state[z] = fwd_out[z]

    other = lambda to: to * 2 + (1 - core)
    sib_own.wait_recv()
    add_gunit(other(y))
    up_bottom.wait_recv()
    sib_down = links.start(whole(down), whole(down), sibling)
    down_top.wait_recv()
    sib_up = links.start(whole(up), whole(up), sibling)

    for copy in out_copies:
        copy.wait_recv()

    def finish_attention(number, _):
        lanes = lanes_of(number)
        carried_in = state[pl.ds(2 * number, 2)].reshape(DH, DH)
        attn = unit[:, lanes] + mask_head[...] * dot(qf[:, lanes], carried_in)
        factor = lax.rsqrt(jnp.mean(attn * attn, axis=1, keepdims=True) + 1e-06)
        scaled = attn * factor
        unit[:, lanes] = scaled
        scale[number] = jnp.broadcast_to(factor, (ROWS, DH))
        normed[:, lanes] = scaled.astype(BF)
        normed_t[lanes_of(number), :] = scaled.T.astype(BF)
        return 0

    lax.fori_loop(0, HEADS, finish_attention, 0, unroll=True)

    def weight_band(band):
        def one_block(which, _):
            block = band * 2 + which
            part = dot(normed_t[0:XROWS, :], og[block]).astype(BF)
            for j in range(4):
                gx[block * 4 + j] = part[:, j * DH : (j + 1) * DH]
            part = dot(normed_t[XROWS:WIDTH, :], og[block]).astype(BF)
            for j in range(4):
                tile = part[:, j * DH : (j + 1) * DH]
                gz[band, which * 4 + j] = tile.reshape(2, ZROWS // 2, DH)
            return 0

        lax.fori_loop(0, 2, one_block, 0, unroll=True)

    ring_x = Ring(links, NX, x, at_x, lambda to: gx.at[pl.ds(to * NZ, NZ)], gx_half, gx_block)
    order = [y, down, up, across]
    rings_z = [
        Ring(links, NZ, z, at_z, lambda to, b=b: gz.at[b, to], gz_half.at[k], gz_block.at[k])
        for k, b in enumerate(order)
    ]
    weight_band(y)
    rings_z[0].begin()
    add_gunit(block_of(down))
    add_gunit(block_of(up))
    sib_down.wait_recv()
    weight_band(down)
    rings_z[1].begin()
    pass_top.wait_recv()
    pass_bottom.wait_recv()
    sib_across = links.start(whole(across), whole(across), sibling)
    sib_up.wait_recv()
    weight_band(up)
    rings_z[2].begin()
    add_gunit(other(down))
    add_gunit(other(up))
    add_gunit(block_of(across))
    sib_across.wait_recv()
    add_gunit(other(across))
    weight_band(across)
    ring_x.begin()
    rings_z[3].begin()

    def grad_attn(number, _):
        lanes = lanes_of(number)
        given, scaled = gunit[:, lanes], unit[:, lanes]
        inner = jnp.mean(given * scaled, axis=1, keepdims=True)
        grad = (scale[number] * (given - scaled * inner)).astype(BF)
        go[:, lanes] = grad
        queries = (qf[:, lanes].astype(F32) * mask_head[...]).astype(BF)
        local = dot(queries, grad, 0, 0)
        bwd_send[pl.ds(2 * number, 2)] = local.astype(BF).reshape(2, DH // 2, DH)
        return 0

    lax.fori_loop(0, HEADS, grad_attn, 0, unroll=True)
    bwd_copies = to_owners(bwd_send, bwd_in)
    bwd_in[z] = bwd_send[z]
    rings_z[0].relay(2)

    ring_y = Ring(links, NY, y, at_y, lambda to: mix.at[to], mix_half, mix_block)
    outward = [across, up, down]

    def project(block, put):
        columns = pl.ds(pl.multiple_of(block * WIDTH, WIDTH), WIDTH)

        def tile(r, _):
            rows = pl.ds(pl.multiple_of(r * half, half), half)
            put(r, dot(normed[rows, :], weight[:, columns]))
            return 0

        lax.fori_loop(0, 2, tile, 0, unroll=True)

    sib_copies = []
    for k, to in enumerate(outward + [y]):

        def put_sib(r, part, k=k):
            sib_send[k, r] = part.astype(BF)

        project(other(to), put_sib)
        sib_copies.append(links.start(sib_send.at[k], sib_recv.at[k], sibling))

    def put_own(k, to):
        sib_copies[k].wait_recv()

        def put(r, part):
            mix[to, r] = (part + sib_recv[k, r].astype(F32)).astype(BF)

        project(block_of(to), put)

    for k, to in enumerate(outward):
        put_own(k, to)
    ring_y.begin()
    rings_z[1].relay(2)
    rings_z[2].relay(2)
    rings_z[0].relay(3)

    for copy in bwd_copies:
        copy.wait_recv()
    run = jnp.zeros((DH // 2, DH), F32)
    suffix = [None] * NZ
    for k in range(NZ - 1, -1, -1):
        suffix[k] = run
        run = bwd_in[k].astype(F32) + same(k, k + 1) * run
    bwd_row[...] = run.astype(BF)
    back_copy = links.start(bwd_row, bwd_rowin, at_x(wrap(x - 1, NX)))
    put_own(3, y)

    rings_z[3].relay(2)
    rings_z[1].relay(3)
    rings_z[2].relay(3)
    rings_z[0].relay(4)
    ring_x.relay(2)

    def backward_local(number, _):
        lanes = lanes_of(number)
        for r in range(ROWS // DH):
            rows, width = slice(r * DH, (r + 1) * DH), (r + 1) * DH
            scores = dot(go[rows, lanes], val[0:width, lanes], 1, 1)
            kept = (scores * allowed[rows, 0:width]).astype(BF)
            gprobs[rows, 0:width] = kept
            gacts[0, rows, lanes] = dot(kept, kf[0:width, lanes])
        for r in range(ROWS // DH):
            rows, below = slice(r * DH, (r + 1) * DH), slice(r * DH, ROWS)
            gacts[1, rows, lanes] = dot(gprobs[below, rows], qf[below, lanes], 0, 0)
            gacts[2, rows, lanes] = dot(probs[number, below, rows], go[below, lanes], 0, 0)
        return 0

    back_copy.wait_recv()
    carried = bwd_rowin[...].astype(F32)
    for k in range(NZ):
        bwd_out[k] = (suffix[k] + same(k + 1, NZ) * carried).astype(BF)
    gout_copies = to_owners(bwd_out, gstate)
    gstate[z] = bwd_out[z]

    lax.fori_loop(0, HEADS, backward_local, 0, unroll=True)
    rings_z[3].relay(3)
    rings_z[1].relay(4)
    rings_z[2].relay(4)

    for copy in gout_copies:
        copy.wait_recv()

    def backward_state(number, _):
        lanes = lanes_of(number)
        carried_in = state[pl.ds(2 * number, 2)].reshape(DH, DH)
        carried_out = gstate[pl.ds(2 * number, 2)].reshape(DH, DH)
        queries, keys, values = qf[:, lanes], kf[:, lanes], val[:, lanes]
        slope = jnp.minimum(queries.astype(F32), 1.0)
        back = mask_head[...] * dot(go[:, lanes], carried_in, 1, 1)
        gacts[0, :, lanes] = (gacts[0, :, lanes] + back) * slope
        slope = jnp.minimum(keys.astype(F32), 1.0)
        back = mask_tail[...] * dot(values, carried_out, 1, 1)
        gacts[1, :, lanes] = (gacts[1, :, lanes] + back) * slope
        back = mask_tail[...] * dot(keys, carried_out)
        gacts[2, :, lanes] = gacts[2, :, lanes] + back
        return 0

    lax.fori_loop(0, HEADS, backward_state, 0, unroll=True)
    grim_copy = links.start(gacts.at[:, pl.ds(0, 8)], grim, token_prev)
    ring_y.relay(2)
    rings_z[3].relay(4)

    def unconvolve(number, _):
        lanes = lanes_of(number)
        for stream in range(3):
            grad = gacts[stream, :, lanes]
            raw = proj[stream, :, lanes].astype(F32)
            both = jnp.concatenate([rim[stream, :, lanes].astype(F32), raw], axis=0)
            acc = taps[stream, 0:1, lanes] * grad
            row = 4 * stream
            tap_part[row : row + 1, lanes] = jnp.sum(grad * raw, axis=0, keepdims=True)
            for j in range(1, KW):
                acc = acc + taps[stream, j : j + 1, lanes] * (
                    pltpu.roll(grad, ROWS - j, 0) * mask_next[j - 1]
                )
                lagged = pltpu.roll(both, j, 0)[EDGE:]
                tap_part[row + j : row + j + 1, lanes] = jnp.sum(
                    grad * mask_back[j - 1] * lagged, axis=0, keepdims=True
                )
            gproj_out[stream, :, lanes] = acc.astype(BF)
        return 0

    tap_part[12:16, :] = jnp.zeros((4, WIDTH), F32)
    lax.fori_loop(0, 2, unconvolve, 0, unroll=True)

    ring_x2 = Ring(links, NZ, z, at_z, lambda to: gx2.at[to], gx2_half, gx2_block)
    ring_z2 = Ring(links, NX, x, at_x, lambda to: gz2.at[to], gz2_half, gz2_block)
    own, first, last = ring_x.finish()
    for k in range(NZ):
        value = own[k].astype(F32) + first[k].astype(F32) + last[k].astype(F32)
        gx2[k] = value.astype(BF).reshape(2, XROWS // 2, DH)
    ring_x2.begin()
    lax.fori_loop(2, HEADS, unconvolve, 0, unroll=True)
    tap_send[...] = tap_part[...].astype(BF)
    tap_copies = [
        links.start(tap_send, tap_in.at[z], at_z(wrap(z + k, NZ))) for k in range(1, NZ)
    ]
    tap_in[z] = tap_send[...]

    ring_x2.relay(2)
    for ring, band in zip(rings_z, order):
        own, first, last = ring.finish()
        for r in range(2):
            value = own[r].astype(F32) + first[r].astype(F32) + last[r].astype(F32)
            gz2[band, r] = value.astype(BF)
    ring_z2.begin()

    grim_copy.wait_recv()

    def unconvolve_rim(number, _):
        lanes = lanes_of(number)
        for stream in range(3):
            grad = gacts[stream, ROWS - EDGE : ROWS, lanes]
            both = jnp.concatenate([grad, grim[stream, :, lanes]], axis=0)
            acc = taps[stream, 0:1, lanes] * grad
            for j in range(1, KW):
                acc = acc + taps[stream, j : j + 1, lanes] * (
                    pltpu.roll(both, EDGE + 8 - j, 0)[0:EDGE]
                    * mask_next[j - 1, ROWS - EDGE : ROWS]
                )
            gproj_out[stream, ROWS - EDGE : ROWS, lanes] = acc.astype(BF)
        return 0

    ring_x2.relay(3)
    lax.fori_loop(0, HEADS, unconvolve_rim, 0, unroll=True)

    ring_z2.relay(2)

    for copy in tap_copies:
        copy.wait_recv()
    summed = tap_in[0].astype(F32)
    for k in range(1, NZ):
        summed = summed + tap_in[k].astype(F32)
    tap_row[...] = summed
    row_copies = [
        links.start(tap_row, tap_rowin.at[x], at_x(wrap(x + k, NX))) for k in range(1, NX)
    ]
    tap_rowin[x] = tap_row[...]

    own, first, last = ring_y.finish()
    for r in range(2):
        value = own[r].astype(F32) + first[r].astype(F32) + last[r].astype(F32)
        mixed_out[r * half : (r + 1) * half, :] = value.astype(BF)
    ring_x2.relay(4)

    for copy in row_copies:
        copy.wait_recv()
    summed = tap_rowin[0]
    for k in range(1, NX):
        summed = summed + tap_rowin[k]
    for stream in range(3):
        gtaps_out[stream] = summed[4 * stream : 4 * stream + 4, :]

    for ring, base, count in ((ring_z2, XROWS, ZROWS // 2), (ring_x2, 0, XROWS // 2)):
        own, first, last = ring.finish()
        for r in range(2):
            value = own[r].astype(F32) + first[r].astype(F32) + last[r].astype(F32)
            gweight_out[base + r * count : base + (r + 1) * count, :] = value
    links.drain()


def hand_over(*refs):
    sources, targets, sems = refs[:4], refs[4:8], refs[8]
    copies = [
        pltpu.make_async_copy(source, target, sems.at[k])
        for k, (source, target) in enumerate(zip(sources, targets))
    ]
    for copy in copies:
        copy.start()
    for copy in copies:
        copy.wait()


def body(projected, conv_weight, out_weight, out_grad, doc_lengths):
    vm = lambda *shape: pltpu.VMEM(shape, BF)
    vf = lambda *shape: pltpu.VMEM(shape, F32)
    piece = (DH // 2, DH)
    hops = lambda n, m, *tile: [vm(2, m // 2, *tile), vm(2, n // 2 - 1, m, *tile)]
    carry = [vm(NZ, *piece), vm(NZ, *piece), vm(*piece), vm(*piece), vm(NZ, *piece), vm(NZ, *piece)]
    scratch = [
        vm(3, ROWS, WIDTH), vm(WIDTH, 8 * WIDTH), vm(8, ROWS, WIDTH), vm(3, EDGE, WIDTH), vf(3, 8, WIDTH),
        vf(3, ROWS, DH), vf(3, ROWS, DH), vf(ROWS, DH), vf(ROWS, DH), vf(ROWS, ROWS),
        vm(ROWS, WIDTH), vm(ROWS, WIDTH), vm(ROWS, WIDTH), vm(HEADS, ROWS, ROWS), vf(ROWS, WIDTH),
        vf(HEADS, ROWS, DH), vf(ROWS, WIDTH), vm(ROWS, WIDTH), vm(WIDTH, ROWS), vm(ROWS, WIDTH),
        vm(ROWS, ROWS), vf(3, ROWS, WIDTH),
        *carry, *carry,
        vm(4, 2, 256, WIDTH), vm(4, 2, 256, WIDTH), vm(4, 2, 256, WIDTH), *hops(NY, 2, 256, WIDTH),
        vm(32, XROWS, DH), *hops(NX, NZ, XROWS, DH),
        vm(NZ, 2, XROWS // 2, DH), *hops(NZ, 2, XROWS // 2, DH),
        vm(NX, NZ, 2, ZROWS // 2, DH), vm(4, 2, 1, ZROWS // 2, DH), vm(4, 2, 3, 2, ZROWS // 2, DH),
        vm(NX, 2, ZROWS // 2, DH), *hops(NX, 2, ZROWS // 2, DH),
        vf(16, WIDTH), vm(16, WIDTH), vm(NZ, 16, WIDTH), vf(16, WIDTH), vf(NX, 16, WIDTH),
        pltpu.SemaphoreType.DMA((3,)), pltpu.SemaphoreType.DMA((COPIES,)), pltpu.SemaphoreType.DMA((COPIES,)),
    ]
    vmem = pl.BlockSpec(memory_space=pltpu.VMEM)
    outside = pl.BlockSpec(memory_space=pl.ANY)
    shapes = (
        jax.ShapeDtypeStruct((ROWS, WIDTH), BF),
        jax.ShapeDtypeStruct((3, ROWS, WIDTH), BF),
        jax.ShapeDtypeStruct((3, KW, WIDTH), F32),
        jax.ShapeDtypeStruct((WIDTH, DH), F32),
    )
    results = pl.pallas_call(
        kernel,
        out_shape=[pltpu.VMEM(shape.shape, shape.dtype) for shape in shapes],
        in_specs=[pl.BlockSpec(memory_space=pltpu.SMEM), outside, vmem, outside, outside],
        out_specs=[vmem] * 4,
        scratch_shapes=scratch,
        compiler_params=pltpu.CompilerParams(
            collective_id=0, has_side_effects=True, vmem_limit_bytes=58 * 2**20
        ),
        cost_estimate=pl.CostEstimate(
            flops=8 * 10**9, bytes_accessed=10**7, transcendentals=10**6
        ),
    )(doc_lengths, projected, conv_weight, out_weight, out_grad)
    return pl.pallas_call(
        hand_over,
        out_shape=shapes,
        in_specs=[outside] * 4,
        out_specs=(outside,) * 4,
        scratch_shapes=[pltpu.SemaphoreType.DMA((4,))],
        compiler_params=pltpu.CompilerParams(vmem_limit_bytes=2**20),
        cost_estimate=pl.CostEstimate(flops=0, bytes_accessed=5 * 10**6, transcendentals=0),
    )(*results)


def solution(mesh):
    return jax.shard_map(
        body,
        mesh=mesh,
        in_specs=(
            P(None, "seq", "head"),
            P(None, None, "head"),
            P("head", None),
            P("seq", "head"),
            P(),
        ),
        out_specs=(
            P("seq", "head"),
            P(None, "seq", "head"),
            P(None, None, "head"),
            P("head", "seq"),
        ),
        check_vma=False,
    )
```
